256 devices in a mesh: group: 16 (over y_hi, x, core), tp: 16 (over y_lo, z).
Axes of the slice: x: 4, y: 4 (y_hi: 2, y_lo: 2; y = y_hi * 2 + y_lo), z: 8, core: 2. Of those that a mesh axis runs over, the one named last changes fastest.
Arguments:
- layer_inputs: bfloat16 [128, 4, 5120], P('group'), may hold values from -6 to 6
- input_norm_gain: bfloat16 [5120], replicated, may hold values from 0.099609375 to 1.8984375
- query_norm_gain: bfloat16 [128], replicated, may hold values from 1 to 2
- key_norm_gain: bfloat16 [128], replicated, may hold values from 1 to 2
- query_matrix: bfloat16 [5120, 4096], P(None, 'tp'), may hold values from -0.078125 to 0.078125
- key_matrix: bfloat16 [5120, 512], P(None, 'tp'), may hold values from -0.078125 to 0.078125
- value_matrix: bfloat16 [5120, 512], P(None, 'tp'), may hold values from -0.078125 to 0.078125
- output_matrix: bfloat16 [4096, 5120], P('tp'), may hold values from -0.09375 to 0.09375
- adapter_down: bfloat16 [5120, 192], P('group', 'tp'), may hold values from -0.078125 to 0.078125
- query_up_factor: bfloat16 [64, 4096], P('group', 'tp'), may hold values from -0.119628906 to 0.119628906
- key_up_factor: bfloat16 [64, 512], P('group', 'tp'), may hold values from -0.119628906 to 0.119628906
- value_up_factor: bfloat16 [64, 512], P('group', 'tp'), may hold values from -0.119628906 to 0.119628906
- output_down_factor: bfloat16 [4096, 64], P('tp', 'group'), may hold values from -0.09375 to 0.09375
- output_up_factor: bfloat16 [64, 5120], P('group', 'tp'), may hold values from -0.119628906 to 0.119628906
- stored_keys: bfloat16 [128, 2048, 512], P('group', 'tp'), may hold values from -120 to 120
- stored_values: bfloat16 [128, 2048, 512], P('group', 'tp'), may hold values from -12 to 12
- filled_lengths: int32 [128], P('group'), may hold values from 1 to 2048, as said below
Outputs:
- attn_output: bfloat16 [128, 4, 5120], P('group', None, 'tp')
The draws below stay inside these ranges and needn't reach their ends.
Inputs may be any that keep to these rules, and one draw needn't show every extreme that they name: `filled_lengths`: some row's cache is full.
All inputs are finite; a program needn't handle non-finite values.
Results may differ from the reference program's by a relative error of at most 0.025.
Values may be sent and summed in bfloat16 or wider, within the bound.
No kernel may reach another device: no remote copies, remote signals or barrier semaphores. Data moves between devices by JAX's collectives and lax.ppermute only.
A program may use at most 128 MiB of HBM per device.

```python
import math
import jax
import jax.numpy as jnp
from jax import lax

MODEL_WIDTH = 5120
QUERY_HEADS = 32
KEY_VALUE_HEADS = 4
HEAD_SIZE = 128
FACTOR_RANK = 64
NEW_TOKENS = 4
CACHE_SLOTS = 2048
TOTAL_ROWS = 128


def draw_stored_keys(key, part):
    key = jax.random.fold_in(key, 11)
    base_weight = jnp.clip(jax.random.normal(key, (TOTAL_ROWS, CACHE_SLOTS, KEY_VALUE_HEADS * HEAD_SIZE), jnp.float32), -4.0, 4.0)
    return base_weight.astype(jnp.bfloat16)


def draw_filled_lengths(key, part):
    key = jax.random.fold_in(key, 12)
    first_key, second_key = jax.random.split(key)
    lengths = jax.random.randint(first_key, (TOTAL_ROWS,), 1, CACHE_SLOTS + 1, dtype=jnp.int32)
    chosen = jax.random.randint(second_key, (), 0, TOTAL_ROWS, dtype=jnp.int32)
    return lengths.at[chosen].set(CACHE_SLOTS).astype(jnp.int32)


def shard_levels(key, dims, pieces, low, largest):
    def one(dim, parts):
        draws = jax.random.uniform(jax.random.fold_in(jax.random.fold_in(key, 6), dim), (parts,), jnp.float32, low / len(pieces), largest / len(pieces))
        return jnp.repeat(jnp.exp(draws), dims[dim] // parts).reshape((-1,) + (1,) * (len(dims) - dim - 1))

    gain = one(*pieces[0])
    for cut in pieces[1:]:
        gain = gain * one(*cut)
    return gain


def centred(own_key, shape, deviation, reach, pieces=(), kind=jnp.bfloat16):
    values = deviation * jax.random.normal(own_key, shape, jnp.float32)
    if pieces:
        values = values * shard_levels(own_key, shape, pieces, -0.22, 0.18)
    return jnp.clip(values, -reach, reach).astype(kind)


def setup_inputs(seed: int = 0) -> dict:
    streams_of = jax.random.split(jax.random.key(seed), 18)
    layer_inputs = centred(streams_of[0], (TOTAL_ROWS, NEW_TOKENS, MODEL_WIDTH), 1.0, 6.0, ((0, 16),))
    input_norm_gain = jnp.clip(1.0 + 0.18 * jax.random.normal(streams_of[1], (MODEL_WIDTH,), jnp.float32), 0.099609375, 1.8984375).astype(jnp.bfloat16)
    query_norm_gain = jnp.clip(jax.random.uniform(streams_of[2], (HEAD_SIZE,), jnp.float32, 1.0, 2.0), 1.0, 2.0).astype(jnp.bfloat16)
    key_norm_gain = jnp.clip(jax.random.uniform(streams_of[3], (HEAD_SIZE,), jnp.float32, 1.0, 2.0), 1.0, 2.0).astype(jnp.bfloat16)
    query_matrix = centred(streams_of[4], (MODEL_WIDTH, QUERY_HEADS * HEAD_SIZE), MODEL_WIDTH ** -0.5, 0.078125, ((1, 16),))
    key_matrix = centred(streams_of[5], (MODEL_WIDTH, KEY_VALUE_HEADS * HEAD_SIZE), MODEL_WIDTH ** -0.5, 0.078125, ((1, 16),))
    value_matrix = centred(streams_of[6], (MODEL_WIDTH, KEY_VALUE_HEADS * HEAD_SIZE), MODEL_WIDTH ** -0.5, 0.078125, ((1, 16),))
    output_matrix = centred(streams_of[7], (QUERY_HEADS * HEAD_SIZE, MODEL_WIDTH), (QUERY_HEADS * HEAD_SIZE) ** -0.5, 0.09375, ((0, 16),))
    adapter_down = centred(streams_of[8], (MODEL_WIDTH, 3 * FACTOR_RANK), MODEL_WIDTH ** -0.5, 0.078125, ((0, 16), (1, 16)))
    query_up_factor = centred(streams_of[9], (FACTOR_RANK, QUERY_HEADS * HEAD_SIZE), 0.02, 0.119628906, ((0, 16), (1, 16)))
    key_up_factor = centred(streams_of[10], (FACTOR_RANK, KEY_VALUE_HEADS * HEAD_SIZE), 0.02, 0.119628906, ((0, 16), (1, 16)))
    value_up_factor = centred(streams_of[11], (FACTOR_RANK, KEY_VALUE_HEADS * HEAD_SIZE), 0.02, 0.119628906, ((0, 16), (1, 16)))
    output_down_factor = centred(streams_of[12], (QUERY_HEADS * HEAD_SIZE, FACTOR_RANK), (QUERY_HEADS * HEAD_SIZE) ** -0.5, 0.09375, ((0, 16), (1, 16)))
    output_up_factor = centred(streams_of[13], (FACTOR_RANK, MODEL_WIDTH), 0.02, 0.119628906, ((0, 16), (1, 16)))
    stored_keys = draw_stored_keys(jax.random.fold_in(streams_of[17], 71), 0)
    stored_values = centred(streams_of[15], (TOTAL_ROWS, CACHE_SLOTS, KEY_VALUE_HEADS * HEAD_SIZE), 2.0, 12.0, ((0, 16), (1, 16)))
    filled_lengths = draw_filled_lengths(jax.random.fold_in(streams_of[17], 71), 0)
    return dict(layer_inputs=layer_inputs, input_norm_gain=input_norm_gain, query_norm_gain=query_norm_gain, key_norm_gain=key_norm_gain, query_matrix=query_matrix, key_matrix=key_matrix, value_matrix=value_matrix, output_matrix=output_matrix, adapter_down=adapter_down, query_up_factor=query_up_factor, key_up_factor=key_up_factor, value_up_factor=value_up_factor, output_down_factor=output_down_factor, output_up_factor=output_up_factor, stored_keys=stored_keys, stored_values=stored_values, filled_lengths=filled_lengths)


EPS = 1e-06
ADAPTER_SCALE = 2.0
THETA = 1000000.0

def rms_scale(values):
    return values * lax.rsqrt(lax.optimization_barrier(jnp.mean(values * values, axis=-1, keepdims=True)) + EPS)

def rotate(heads, positions):
    half_dim = heads.shape[-1] // 2
    inverse = THETA ** (-(jnp.arange(half_dim, dtype=jnp.float32) * 2.0 / heads.shape[-1]))
    angles = positions[..., None, None] * inverse
    cosines = jnp.cos(angles)
    sines = jnp.sin(angles)
    leading = heads[..., :half_dim]
    trailing = heads[..., half_dim:]
    return jnp.concatenate([leading * cosines - trailing * sines, trailing * cosines + leading * sines], axis=-1)

def merge_adapter(base_weight, lower, upper):
    weight_update = jnp.dot(lower, upper, preferred_element_type=jnp.float32)
    return (base_weight.astype(jnp.float32) + ADAPTER_SCALE * weight_update).astype(jnp.bfloat16)

def project(layer_inputs, input_norm_gain, query_norm_gain, query_merged_weight, key_merged_weight, value_merged_weight, lengths):
    rows_here, step_count, width = layer_inputs.shape
    head_dim = query_norm_gain.shape[0]
    flat = layer_inputs.astype(jnp.float32).reshape(rows_here * step_count, width)
    normed = (rms_scale(flat) * input_norm_gain.astype(jnp.float32)).astype(jnp.bfloat16)
    positions = (lengths[:, None] + jnp.arange(step_count, dtype=jnp.int32)[None, :]).astype(jnp.float32)
    raw_queries = jnp.dot(normed, query_merged_weight, preferred_element_type=jnp.float32).reshape(rows_here, step_count, -1, head_dim)
    queries = rotate(rms_scale(raw_queries) * query_norm_gain.astype(jnp.float32), positions)
    queries = queries.astype(jnp.bfloat16).reshape(rows_here, step_count, -1)
    raw_keys = jnp.dot(normed, key_merged_weight, preferred_element_type=jnp.float32).astype(jnp.bfloat16).reshape(rows_here, step_count, -1)
    new_values = jnp.dot(normed, value_merged_weight, preferred_element_type=jnp.float32).astype(jnp.bfloat16).reshape(rows_here, step_count, -1)
    return (queries, raw_keys, new_values, positions)

def finish_keys(raw_keys, positions, head_dim, key_norm_gain):
    rows_here, step_count, _ = raw_keys.shape
    heads = raw_keys.astype(jnp.float32).reshape(rows_here, step_count, -1, head_dim)
    return rotate(rms_scale(heads) * key_norm_gain.astype(jnp.float32), positions).astype(jnp.bfloat16).reshape(rows_here, step_count, -1)

def attend_row(items):
    row_queries, row_new_keys, row_new_values, row_cached_keys, row_cached_values, length = items
    joined_keys = jnp.concatenate([row_cached_keys, row_new_keys], axis=0).astype(jnp.float32).reshape(-1, KEY_VALUE_HEADS, HEAD_SIZE)
    joined_values = jnp.concatenate([row_cached_values, row_new_values], axis=0).astype(jnp.float32).reshape(-1, KEY_VALUE_HEADS, HEAD_SIZE)
    query_groups = row_queries.astype(jnp.float32).reshape(NEW_TOKENS, KEY_VALUE_HEADS, QUERY_HEADS // KEY_VALUE_HEADS, HEAD_SIZE)
    scores = jnp.einsum('sngd,knd->ngsk', query_groups, joined_keys) / math.sqrt(HEAD_SIZE)
    position = jnp.arange(CACHE_SLOTS + NEW_TOKENS, dtype=jnp.int32)
    in_cache = position < length
    causal = position[None, :] - CACHE_SLOTS <= jnp.arange(NEW_TOKENS, dtype=jnp.int32)[:, None]
    usable = jnp.where(position[None, :] < CACHE_SLOTS, in_cache[None, :], causal)
    masked = jnp.where(usable, scores, -1e+30)
    maxima = lax.optimization_barrier(jnp.max(masked, axis=-1, keepdims=True))
    weights = jnp.where(usable, jnp.exp(masked - maxima), 0.0).astype(jnp.bfloat16)
    totals = lax.optimization_barrier(jnp.sum(weights.astype(jnp.float32), axis=-1))
    weighted = jnp.einsum('ngsk,knd->ngsd', weights.astype(jnp.float32), joined_values)
    heads_out = (weighted / totals[..., None]).astype(jnp.bfloat16)
    return heads_out.transpose(2, 0, 1, 3).reshape(NEW_TOKENS, QUERY_HEADS * HEAD_SIZE)

def reference(layer_inputs, input_norm_gain, query_norm_gain, key_norm_gain, query_matrix, key_matrix, value_matrix, output_matrix, adapter_down, query_up_factor, key_up_factor, value_up_factor, output_down_factor, output_up_factor, stored_keys, stored_values, filled_lengths):
    factor_rank = query_up_factor.shape[0]
    query_merged_weight = merge_adapter(query_matrix, adapter_down[:, :factor_rank], query_up_factor)
    key_merged_weight = merge_adapter(key_matrix, adapter_down[:, factor_rank:2 * factor_rank], key_up_factor)
    value_merged_weight = merge_adapter(value_matrix, adapter_down[:, 2 * factor_rank:], value_up_factor)
    merged_output = merge_adapter(output_matrix, output_down_factor, output_up_factor)
    head_dim = query_norm_gain.shape[0]
    queries, raw_keys, new_values, positions = project(layer_inputs, input_norm_gain, query_norm_gain, query_merged_weight, key_merged_weight, value_merged_weight, filled_lengths)
    new_keys = finish_keys(raw_keys, positions, head_dim, key_norm_gain)
    attended = lax.map(attend_row, (queries, new_keys, new_values, stored_keys, stored_values, filled_lengths))
    rows_all, step_count, _ = layer_inputs.shape
    output = jnp.dot(attended.reshape(rows_all * step_count, -1), merged_output, preferred_element_type=jnp.float32)
    return output.reshape(rows_all, step_count, -1).astype(jnp.bfloat16)
```

```python
import functools
import math

import jax
import jax.numpy as jnp
import numpy as np
from jax import lax
from jax.experimental import pallas as pl
from jax.experimental.pallas import tpu as pltpu
from jax.sharding import PartitionSpec as P

EPS = 1e-06
ADAPTER_SCALE = 2.0
THETA = 1000000.0
PARTS = 16
HEAD = 128
TOKENS = 4
ROWS = 8
F32 = jnp.float32
BF16 = jnp.bfloat16


def call(body, out_shapes, *args, smem=(), flops=0, moved=0):
    specs = [
        pl.BlockSpec(memory_space=pltpu.SMEM if i in smem else pltpu.VMEM)
        for i in range(len(args))
    ]
    return pl.pallas_call(
        body,
        out_shape=out_shapes,
        in_specs=specs,
        out_specs=jax.tree.map(lambda _: pl.BlockSpec(memory_space=pltpu.VMEM), out_shapes),
        compiler_params=pltpu.CompilerParams(vmem_limit_bytes=24 * 2**20),
        cost_estimate=pl.CostEstimate(flops=flops, bytes_accessed=moved, transcendentals=0),
    )(*args)


def dot(a, b, contract=(1, 0)):
    return lax.dot_general(
        a, b, (((contract[0],), (contract[1],)), ((), ())), preferred_element_type=F32
    )


def widen(block, lanes):
    return jnp.concatenate(
        [block, jnp.zeros((block.shape[0], lanes - block.shape[1]), block.dtype)], axis=1
    )


def pack_body(down, out_down, query_up, key_up, value_up, out_up, packed):
    f = lambda ref: ref[...].astype(F32)
    up = jnp.concatenate([f(query_up), f(key_up), f(value_up)], axis=1)
    block = jnp.concatenate(
        [widen(f(down), 384), widen(f(out_down), 384), widen(up, 384), widen(f(out_up), 384)],
        axis=0,
    ).astype(BF16)
    for i in range(PARTS):
        packed[i] = block


def project_body(x_ref, gain, query_w, key_w, value_w, packed, low, base, ups, out_down, out_up):
    x = x_ref[...].astype(F32)
    scale = lax.rsqrt(jnp.mean(x * x, axis=-1, keepdims=True) + EPS)
    normed = (x * scale * gain[...].astype(F32)).astype(BF16)
    pieces = [packed[i].astype(F32) for i in range(PARTS)]
    down = jnp.concatenate([p[0:16, 0:320] for p in pieces], axis=1).astype(BF16)
    low_here = dot(normed, down, (1, 1))
    lane = lax.broadcasted_iota(jnp.int32, low_here.shape, 1)
    low_here = jnp.where(lane < 12, low_here, 0.0)
    block = widen(low_here, 128).astype(BF16)
    for i in range(PARTS):
        low[i] = block
    base[:, 0:256] = dot(normed, query_w[...])
    both = jnp.concatenate([key_w[...], value_w[...]], axis=0)
    base[:, 256:384] = widen(dot(normed, both, (1, 1)), 128)
    out_down[...] = jnp.concatenate([p[12:16, 0:256] for p in pieces], axis=0).astype(BF16)
    ups[...] = jnp.concatenate([p[16:20] for p in pieces], axis=0).astype(BF16)
    out_up[...] = jnp.concatenate([p[20:24] for p in pieces], axis=0).astype(BF16)


def rms_rope(heads, gain, cosines, sines):
    scale = lax.rsqrt(jnp.mean(heads * heads, axis=-1, keepdims=True) + EPS)
    heads = heads * scale * gain
    return heads * cosines + pltpu.roll(heads, 64, 1) * sines


def regroup(count_from, count_to):
    row = lax.broadcasted_iota(jnp.int32, (64, 64), 0)
    col = lax.broadcasted_iota(jnp.int32, (64, 64), 1)
    source = ((row // TOKENS) % count_to) * (count_from * TOKENS)
    source = source + (row // (TOKENS * count_to)) * TOKENS + row % TOKENS
    return jnp.where(col == source, 1.0, 0.0).astype(BF16)


def query_body(low, base, ups, cosines, sines, gain, packed):
    first = jnp.zeros((32, 128), F32)
    second = jnp.zeros((32, 128), F32)
    lane = lax.broadcasted_iota(jnp.int32, (32, 128), 1)
    for t in range(PARTS):
        start = 12 * t
        piece = low[t].astype(F32)
        piece = pltpu.roll(piece, start % 128, 1) if start % 128 else piece
        if start + 12 <= 128:
            first = first + piece
        elif start >= 128:
            second = second + piece
        else:
            first = first + jnp.where(lane >= start, piece, 0.0)
            second = second + jnp.where(lane < start, piece, 0.0)
    lift = ups[...]
    column = lax.broadcasted_iota(jnp.int32, lift.shape, 1)
    zero = jnp.zeros_like(lift)
    lift_query = jnp.where(column < 256, lift, zero)
    lift_key = jnp.where((column >= 256) & (column < 288), lift, zero)
    lift_value = jnp.where((column >= 288) & (column < 320), lift, zero)
    update = dot(first.astype(BF16), jnp.concatenate([lift_query, lift_key], axis=0))
    update = update + dot(
        second.astype(BF16), jnp.concatenate([lift_value, jnp.zeros_like(lift_value)], axis=0)
    )
    raw = base[...] + ADAPTER_SCALE * update
    heads = [
        rms_rope(raw[:, j * HEAD : (j + 1) * HEAD], gain[...], cosines[...], sines[...])
        for j in range(2)
    ]
    queries = jnp.concatenate(heads, axis=0).astype(BF16)
    queries = dot(regroup(8, 2), queries).astype(BF16)
    fresh = raw[:, 256:384]
    fold = jnp.where(lane[0:16] < 64, fresh[0:16], pltpu.roll(fresh[16:32], 64, 1))
    block = jnp.concatenate([queries, fold.astype(BF16)], axis=0)
    for i in range(PARTS):
        packed[i] = block


def softmax_parts(scores, usable):
    masked = jnp.where(usable, scores, -1e30)
    highest = jnp.max(masked, axis=-1, keepdims=True).astype(BF16).astype(F32)
    weights = jnp.where(usable, jnp.exp(masked - highest), 0.0).astype(BF16)
    total = jnp.sum(weights.astype(F32), axis=-1, keepdims=True)
    return highest, weights, total


def attend_body(
    me, lengths, gathered, keys, values, cosines, sines, gain, packed, own_weighted, own_stats
):
    mine = me[0]
    offset = mine * 128
    scaling = 1.0 / math.sqrt(HEAD)
    everything = [gathered[t, 0:64].astype(F32) for t in range(PARTS)]
    lane = lax.broadcasted_iota(jnp.int32, (128, 128), 1)
    stats = jnp.zeros((128, 128), F32)
    held = None
    for b in range(ROWS):
        queries = jnp.concatenate(
            [everything[t][b * 8 : (b + 1) * 8] for t in range(PARTS)], axis=0
        ).astype(BF16)
        scores = jnp.concatenate(
            [
                dot(queries[n * 32 : (n + 1) * 32], keys[b, :, n * HEAD : (n + 1) * HEAD], (1, 1))
                for n in range(4)
            ],
            axis=0,
        )
        usable = lane + offset < lengths[b]
        highest, weights, total = softmax_parts(scores * scaling, usable)
        total_high = total.astype(BF16).astype(F32)
        stats = jnp.where(lane == b, highest, stats)
        stats = jnp.where(lane == 8 + b, total_high, stats)
        stats = jnp.where(lane == 16 + b, total - total_high, stats)
        weighted = [
            dot(weights[n * 32 : (n + 1) * 32], values[b, :, n * HEAD : (n + 1) * HEAD])
            for n in range(4)
        ]
        if b % 2 == 0:
            held = weighted
            continue
        for t in range(PARTS):
            rows = slice(t % 4 * 8, t % 4 * 8 + 8)
            pair = jnp.concatenate([held[t // 4][rows], weighted[t // 4][rows]], axis=0)
            packed[t, (b - 1) * 8 : (b + 1) * 8] = pair.astype(BF16)
    for t in range(PARTS):
        packed[t, 64:80] = jnp.concatenate(
            [stats[t * 8 : (t + 1) * 8], jnp.zeros((8, 128), F32)], axis=0
        ).astype(BF16)

    first = (mine // 4) * 4
    fresh_key = []
    fresh_value = []
    for q in range(4):
        fold = gathered[first + q, 64:80].astype(F32)
        wide = jnp.concatenate([fold, pltpu.roll(fold, 64, 1)], axis=0)
        fresh_key.append(wide[:, 0:32])
        fresh_value.append(wide[:, 32:64])
    new_keys = jnp.concatenate(fresh_key, axis=1).astype(BF16).astype(F32)
    new_keys = rms_rope(new_keys, gain[...], cosines[...], sines[...]).astype(BF16)
    new_values = jnp.concatenate(fresh_value, axis=1).astype(BF16)
    own = gathered[mine, 0:64]
    scores = dot(own, new_keys, (1, 1)) * scaling
    row = lax.broadcasted_iota(jnp.int32, (64, 32), 0)
    col = lax.broadcasted_iota(jnp.int32, (64, 32), 1)
    usable = (row // 8 == col // TOKENS) & (col % TOKENS <= row % TOKENS)
    highest, weights, total = softmax_parts(scores, usable)
    own_weighted[...] = dot(weights, new_values)
    lane = lax.broadcasted_iota(jnp.int32, (8, 128), 1)
    stats = jnp.zeros((8, 128), F32)
    for b in range(ROWS):
        stats = jnp.where(lane == b, highest[b * 8 : (b + 1) * 8], stats)
        stats = jnp.where(lane == 8 + b, total[b * 8 : (b + 1) * 8], stats)
    own_stats[...] = stats


def output_body(gathered, own_weighted, own_stats, output_w, out_down, packed):
    blocks = [gathered[t].astype(F32) for t in range(PARTS)]
    stats = [block[64:72] for block in blocks] + [own_stats[...]]
    values = [block[0:64] for block in blocks] + [own_weighted[...]]
    highest = functools.reduce(jnp.maximum, stats)
    factors = [jnp.exp(jnp.minimum(s - highest, 0.0)) for s in stats]
    total = jnp.zeros((8, 128), F32)
    for s, f in zip(stats, factors):
        total = total + f * (pltpu.roll(s, 120, 1) + pltpu.roll(s, 112, 1))
    lane = lax.broadcasted_iota(jnp.int32, (8, 128), 1)
    inverse = 1.0 / jnp.where(lane < 8, total, 1.0)
    pieces = []
    for b in range(ROWS):
        piece = jnp.zeros((8, 128), F32)
        for v, f in zip(values, factors):
            piece = piece + f[:, b : b + 1] * v[b * 8 : (b + 1) * 8]
        pieces.append(piece * inverse[:, b : b + 1])
    heads = jnp.concatenate(pieces, axis=0).astype(BF16)
    heads = dot(regroup(2, 8), heads).astype(BF16)
    heads = jnp.concatenate([heads[0:32], heads[32:64]], axis=1)
    low = dot(heads, out_down[...], (1, 1))
    partial = dot(heads, output_w[...])
    for t in range(PARTS):
        packed[t] = jnp.concatenate([partial[:, t * 320 : (t + 1) * 320], low], axis=1).astype(
            BF16
        )


def finish_body(gathered, out_up, result):
    total = gathered[0].astype(F32)
    for t in range(1, PARTS):
        total = total + gathered[t].astype(F32)
    update = dot(total[:, 320:384].astype(BF16), out_up[...])
    out = total[:, 0:320] + ADAPTER_SCALE * update[:, 0:320]
    result[...] = out.astype(BF16)


def swap(block, axis):
    return lax.all_to_all(block, axis, 0, 0)


def local(
    layer_inputs,
    input_norm_gain,
    query_norm_gain,
    key_norm_gain,
    query_matrix,
    key_matrix,
    value_matrix,
    output_matrix,
    adapter_down,
    query_up_factor,
    key_up_factor,
    value_up_factor,
    output_down_factor,
    output_up_factor,
    stored_keys,
    stored_values,
    filled_lengths,
):
    shape = jax.ShapeDtypeStruct
    packed = call(
        pack_body,
        shape((PARTS, 24, 384), BF16),
        adapter_down.T,
        output_down_factor.T,
        query_up_factor,
        key_up_factor,
        value_up_factor,
        output_up_factor,
    )
    packed = swap(packed, "group")
    low, base, ups, out_down, out_up = call(
        project_body,
        (
            shape((PARTS, 32, 128), BF16),
            shape((32, 384), F32),
            shape((64, 384), BF16),
            shape((64, 256), BF16),
            shape((64, 384), BF16),
        ),
        layer_inputs.reshape(ROWS * TOKENS, -1),
        input_norm_gain.reshape(1, -1),
        query_matrix,
        key_matrix.T,
        value_matrix.T,
        packed,
    )
    low = swap(low, "tp")
    inverse = THETA ** (-(np.arange(64, dtype=np.float64) * 2.0 / HEAD))
    positions = filled_lengths[:, None] + jnp.arange(TOKENS, dtype=jnp.int32)[None, :]
    angles = positions.astype(F32).reshape(-1, 1) * jnp.asarray(inverse, F32)
    cosines = jnp.cos(angles)
    sines = jnp.sin(angles)
    cosines = jnp.concatenate([cosines, cosines], axis=1)
    sines = jnp.concatenate([-sines, sines], axis=1)
    queries = call(
        query_body,
        shape((PARTS, 80, 128), BF16),
        low,
        base,
        ups,
        cosines,
        sines,
        query_norm_gain.astype(F32).reshape(1, -1),
    )
    queries = swap(queries, "tp")
    me = lax.axis_index("tp").astype(jnp.int32).reshape(1)
    parts, own_weighted, own_stats = call(
        attend_body,
        (shape((PARTS, 80, 128), BF16), shape((64, 128), F32), shape((8, 128), F32)),
        me,
        filled_lengths,
        queries,
        stored_keys,
        stored_values,
        cosines,
        sines,
        key_norm_gain.astype(F32).reshape(1, -1),
        smem=(0, 1),
    )
    parts = swap(parts, "tp")
    partial = call(
        output_body,
        shape((PARTS, 32, 384), BF16),
        parts,
        own_weighted,
        own_stats,
        output_matrix,
        out_down,
    )
    partial = swap(partial, "tp")
    result = call(finish_body, shape((32, 320), BF16), partial, out_up)
    return result.reshape(ROWS, TOKENS, 320)


def solution(mesh):
    in_specs = (
        P("group", None, None),
        P(),
        P(),
        P(),
        P(None, "tp"),
        P(None, "tp"),
        P(None, "tp"),
        P("tp", None),
        P("group", "tp"),
        P("group", "tp"),
        P("group", "tp"),
        P("group", "tp"),
        P("tp", "group"),
        P("group", "tp"),
        P("group", "tp", None),
        P("group", "tp", None),
        P("group"),
    )
    out_specs = P("group", None, "tp")
    return jax.shard_map(local, mesh=mesh, in_specs=in_specs, out_specs=out_specs, check_vma=False)
```

```python
import functools
import math

import jax
import jax.numpy as jnp
import numpy as np
from jax import lax
from jax.experimental import pallas as pl
from jax.experimental.pallas import tpu as pltpu
from jax.sharding import Mesh
from jax.sharding import PartitionSpec as P

EPS = 1e-06
ADAPTER_SCALE = 2.0
THETA = 1000000.0
GROUPS = 16
PARTS = 16
TP = ("far", "near")
HEAD = 128
TOKENS = 4
ROWS = 8
F32 = jnp.float32
BF16 = jnp.bfloat16
SHAPE = jax.ShapeDtypeStruct
WINDOW = 16 * 2**20


def call(body, out_shapes, args, spaces, room, scratch=(), left=(), moved=0):
    places = {"s": pltpu.SMEM, "a": pltpu.HBM, "v": pltpu.VMEM}
    specs = [pl.BlockSpec(memory_space=places[c]) for c in spaces]
    many = isinstance(out_shapes, tuple)
    outs = [
        pl.BlockSpec(memory_space=pltpu.HBM if i in left else pltpu.VMEM)
        for i in range(len(out_shapes) if many else 1)
    ]
    return pl.pallas_call(
        body,
        out_shape=out_shapes,
        in_specs=specs,
        out_specs=tuple(outs) if many else outs[0],
        scratch_shapes=list(scratch),
        compiler_params=pltpu.CompilerParams(vmem_limit_bytes=int((64 - room) * 2**20)),
        cost_estimate=pl.CostEstimate(flops=0, bytes_accessed=moved, transcendentals=0),
    )(*args)


def dot(a, b, contract=(1, 0)):
    return lax.dot_general(
        a, b, (((contract[0],), (contract[1],)), ((), ())), preferred_element_type=F32
    )


def widen(block, lanes):
    return jnp.concatenate(
        [block, jnp.zeros((block.shape[0], lanes - block.shape[1]), block.dtype)], axis=1
    )


def iotas(shape):
    return [lax.broadcasted_iota(jnp.int32, shape, d) for d in range(2)]


def fetch(sources, held, sems):
    copies = [pltpu.make_async_copy(s, h, sems.at[i]) for i, (s, h) in enumerate(zip(sources, held))]
    for copy in copies:
        copy.start()
    return copies


def pack_body(*refs):
    packed, held = refs[6], refs[7:13]
    for copy in fetch(refs[:6], held, refs[13]):
        copy.wait()
    down, out_down, query_up, key_up, value_up, out_up = [h[...].astype(F32) for h in held]
    up = jnp.concatenate([query_up, key_up, value_up], axis=1)
    block = jnp.concatenate(
        [widen(down, 384), widen(out_down, 384), widen(up, 384), widen(out_up, 384)], axis=0
    ).astype(BF16)
    for i in range(GROUPS):
        packed[i] = block


def normed_body(
    lengths, x_any, gain_any, inverse_any, normed, cosines, sines, x_ref, gain, inverse, sems
):
    for copy in fetch((x_any, gain_any, inverse_any), (x_ref, gain, inverse), sems):
        copy.wait()
    x = x_ref[...].astype(F32).reshape(ROWS * TOKENS, -1)
    scale = lax.rsqrt(jnp.mean(x * x, axis=-1, keepdims=True) + EPS)
    normed[...] = (x * scale * gain[...].astype(F32).reshape(1, -1)).astype(BF16)
    row, lane = iotas((ROWS * TOKENS, HEAD))
    position = row % TOKENS
    for b in range(ROWS):
        position = position + jnp.where(row // TOKENS == b, lengths[b], 0)
    angles = position.astype(F32) * inverse[...]
    cosines[...] = jnp.cos(angles)
    sines[...] = jnp.where(lane < 64, -1.0, 1.0) * jnp.sin(angles)


def low_body(packed, normed, low):
    pieces = [packed[g, 0:16, 0:320].astype(F32) for g in range(GROUPS)]
    down = jnp.concatenate(pieces, axis=1).astype(BF16)
    block = widen(dot(down, normed[...], (1, 1)), 128).astype(BF16)
    for t in range(PARTS):
        low[t] = block


CHUNKS = 4


def base_body(
    packed, normed, query_any, key_any, value_any, base, ups, out_down, out_up,
    query_w, key_w, value_w, sems,
):
    step = query_any.shape[0] // CHUNKS
    rows = [pl.ds(c * step, step) for c in range(CHUNKS)]
    copies = fetch(
        [query_any.at[r] for r in rows] + [key_any, value_any],
        [query_w.at[r] for r in rows] + [key_w, value_w],
        sems,
    )
    pieces = [packed[g].astype(F32) for g in range(GROUPS)]
    out_down[...] = jnp.concatenate([p[12:16, 0:256] for p in pieces], axis=0).astype(BF16)
    ups[...] = jnp.concatenate([p[16:20] for p in pieces], axis=0).astype(BF16)
    out_up[...] = jnp.concatenate([p[20:24] for p in pieces], axis=0).astype(BF16)
    value = normed[...]
    raw = jnp.zeros((32, 256), F32)
    for c in range(CHUNKS):
        copies[c].wait()
        part = slice(c * step, (c + 1) * step)
        raw = raw + dot(value[:, part], query_w[part, :])
    base[:, 0:256] = raw
    copies[CHUNKS].wait()
    copies[CHUNKS + 1].wait()
    both = jnp.concatenate([key_w[...], value_w[...]], axis=0)
    base[:, 256:384] = widen(dot(value, both, (1, 1)), 128)


def rms_rope(heads, gain, cosines, sines):
    scale = lax.rsqrt(jnp.mean(heads * heads, axis=-1, keepdims=True) + EPS)
    heads = heads * scale * gain
    return heads * cosines + pltpu.roll(heads, 64, 1) * sines


def regroup(count_from, count_to):
    row, col = iotas((64, 64))
    source = ((row // TOKENS) % count_to) * (count_from * TOKENS)
    source = source + (row // (TOKENS * count_to)) * TOKENS + row % TOKENS
    return jnp.where(col == source, 1.0, 0.0).astype(BF16)


def query_body(low, base, ups, cosines, sines, gain, packed, own, fresh):
    ranks = jnp.concatenate([low[t].astype(F32)[0:12] for t in range(PARTS)], axis=0)
    ranks = ranks[:, 0:32].astype(BF16)
    lift = ups[...]
    _, column = iotas(lift.shape)
    zero = jnp.zeros_like(lift)
    lifts = [
        jnp.where((column >= first) & (column < last), lift, zero)
        for first, last in ((0, 256), (256, 288), (288, 320))
    ]
    update = dot(ranks, jnp.concatenate(lifts, axis=0), (0, 0))
    raw = base[...] + ADAPTER_SCALE * update
    scale = gain[...].astype(F32).reshape(1, -1)
    heads = [
        rms_rope(raw[:, j * HEAD : (j + 1) * HEAD], scale, cosines[...], sines[...])
        for j in range(2)
    ]
    queries = jnp.concatenate(heads, axis=0).astype(BF16)
    queries = dot(regroup(8, 2), queries).astype(BF16)
    for i in range(PARTS):
        packed[i] = queries
    own[...] = queries
    _, lane = iotas((16, 128))
    folded = jnp.where(lane < 64, raw[0:16, 256:384], pltpu.roll(raw[16:32, 256:384], 64, 1))
    fresh[...] = folded.astype(BF16)


def softmax_parts(scores, usable):
    masked = jnp.where(usable, scores, -1e30)
    highest = jnp.max(masked, axis=-1, keepdims=True).astype(BF16).astype(F32)
    weights = jnp.where(usable, jnp.exp(masked - highest), 0.0).astype(BF16)
    total = jnp.sum(weights.astype(F32), axis=-1, keepdims=True)
    return highest, weights, total


SCALING = 1.0 / math.sqrt(HEAD)
SPAN = 128


def attend_body(place, lengths, gathered, keys, values, packed):
    offset = place[0] * SPAN
    everything = [gathered[t].astype(F32) for t in range(PARTS)]
    _, lane = iotas((128, 128))
    stats = jnp.zeros((128, 128), F32)
    found = []
    for b in range(ROWS):
        query = jnp.concatenate(
            [q[b * 8 : (b + 1) * 8] for q in everything], axis=0
        ).astype(BF16)
        scores = jnp.concatenate(
            [
                dot(query[n * 32 : (n + 1) * 32], keys[b, :, n * HEAD : (n + 1) * HEAD], (1, 1))
                for n in range(4)
            ],
            axis=0,
        )
        highest, weights, total = softmax_parts(scores * SCALING, lane + offset < lengths[b])
        total_high = total.astype(BF16).astype(F32)
        stats = jnp.where(lane == b, highest, stats)
        stats = jnp.where(lane == 8 + b, total_high, stats)
        stats = jnp.where(lane == 16 + b, total - total_high, stats)
        found.append(
            [
                dot(weights[n * 32 : (n + 1) * 32], values[b, :, n * HEAD : (n + 1) * HEAD])
                for n in range(4)
            ]
        )
    for t in range(PARTS):
        rows = slice(t % 4 * 8, t % 4 * 8 + 8)
        block = [found[b][t // 4][rows] for b in range(ROWS)] + [stats[t * 8 : (t + 1) * 8]]
        packed[t] = jnp.concatenate(block, axis=0).astype(BF16)


def fresh_body(
    place, near, near_1, near_2, near_3, own, cosines, sines, gain, weighted, stats_out, gathered
):
    for k, piece in enumerate((near, near_1, near_2, near_3)):
        gathered[(place[0] % 4) ^ k] = piece[...].astype(F32)
    fresh_key = []
    fresh_value = []
    for q in range(4):
        fold = gathered[q]
        wide = jnp.concatenate([fold, pltpu.roll(fold, 64, 1)], axis=0)
        fresh_key.append(wide[:, 0:32])
        fresh_value.append(wide[:, 32:64])
    new_keys = jnp.concatenate(fresh_key, axis=1)
    scale = gain[...].astype(F32).reshape(1, -1)
    new_keys = rms_rope(new_keys, scale, cosines[...], sines[...]).astype(BF16)
    new_values = jnp.concatenate(fresh_value, axis=1).astype(BF16)
    scores = dot(own[...], new_keys, (1, 1)) * SCALING
    row, col = iotas((64, 32))
    usable = (row // 8 == col // TOKENS) & (col % TOKENS <= row % TOKENS)
    highest, weights, total = softmax_parts(scores, usable)
    weighted[...] = dot(weights, new_values)
    _, lane = iotas((8, 128))
    stats = jnp.zeros((8, 128), F32)
    for b in range(ROWS):
        stats = jnp.where(lane == b, highest[b * 8 : (b + 1) * 8], stats)
        stats = jnp.where(lane == 8 + b, total[b * 8 : (b + 1) * 8], stats)
    stats_out[...] = stats


def output_body(
    gathered, own_weighted, own_stats, output_any, out_down, packed, output_w, sems
):
    step = output_any.shape[1] // CHUNKS
    parts = [pl.ds(c * step, step) for c in range(CHUNKS)]
    copies = fetch(
        [output_any.at[:, part] for part in parts], [output_w.at[:, part] for part in parts], sems
    )
    blocks = [gathered[t].astype(F32) for t in range(PARTS)]
    stats = [block[64:72] for block in blocks] + [own_stats[...]]
    values = [block[0:64] for block in blocks] + [own_weighted[...]]
    highest = functools.reduce(jnp.maximum, stats)
    factors = [jnp.exp(jnp.minimum(s - highest, 0.0)) for s in stats]
    total = jnp.zeros((8, 128), F32)
    for s, f in zip(stats, factors):
        total = total + f * (pltpu.roll(s, 120, 1) + pltpu.roll(s, 112, 1))
    _, lane = iotas((8, 128))
    inverse = 1.0 / jnp.where(lane < 8, total, 1.0)
    pieces = []
    for b in range(ROWS):
        piece = jnp.zeros((8, 128), F32)
        for v, f in zip(values, factors):
            piece = piece + f[:, b : b + 1] * v[b * 8 : (b + 1) * 8]
        pieces.append(piece * inverse[:, b : b + 1])
    heads = jnp.concatenate(pieces, axis=0).astype(BF16)
    heads = dot(regroup(2, 8), heads).astype(BF16)
    heads = jnp.concatenate([heads[0:32], heads[32:64]], axis=1)
    low = dot(heads, out_down[...], (1, 1))
    share = PARTS // CHUNKS
    for c in range(CHUNKS):
        copies[c].wait()
        partial = dot(heads, output_w[:, c * step : (c + 1) * step])
        for t in range(share):
            block = jnp.concatenate([partial[:, t * 320 : (t + 1) * 320], low], axis=1)
            packed[c * share + t] = block.astype(BF16)


def finish_body(gathered, out_up, result):
    total = gathered[0].astype(F32)
    for t in range(1, PARTS):
        total = total + gathered[t].astype(F32)
    update = dot(total[:, 320:384].astype(BF16), out_up[...])
    out = total[:, 0:320] + ADAPTER_SCALE * update[:, 0:320]
    result[...] = out.reshape(ROWS, TOKENS, 320).astype(BF16)


def swap(block, axis):
    return lax.all_to_all(block, axis, 0, 0)


def local(
    layer_inputs,
    input_norm_gain,
    query_norm_gain,
    key_norm_gain,
    query_matrix,
    key_matrix,
    value_matrix,
    output_matrix,
    adapter_down,
    query_up_factor,
    key_up_factor,
    value_up_factor,
    output_down_factor,
    output_up_factor,
    stored_keys,
    stored_values,
    filled_lengths,
):
    dma = pltpu.SemaphoreType.DMA
    width = layer_inputs.shape[-1]
    place = lax.axis_index(TP).astype(jnp.int32).reshape(1)
    shards = (
        adapter_down.T,
        output_down_factor.T,
        query_up_factor,
        key_up_factor,
        value_up_factor,
        output_up_factor,
    )
    packed = call(
        pack_body,
        SHAPE((GROUPS, 24, 384), BF16),
        shards,
        "aaaaaa",
        8,
        [pltpu.VMEM(s.shape, BF16) for s in shards] + [dma((6,))],
    )
    packed = swap(packed, "group")

    inverse = THETA ** (-(np.arange(64, dtype=np.float64) * 2.0 / HEAD))
    inverse = jnp.asarray(np.concatenate([inverse, inverse]).reshape(1, HEAD), F32)
    normed, cosines, sines = call(
        normed_body,
        (SHAPE((32, width), BF16), SHAPE((32, HEAD), F32), SHAPE((32, HEAD), F32)),
        (filled_lengths, layer_inputs, input_norm_gain, inverse),
        "saaa",
        12,
        [
            pltpu.VMEM(layer_inputs.shape, BF16),
            pltpu.VMEM((width,), BF16),
            pltpu.VMEM((1, HEAD), F32),
            dma((3,)),
        ],
        moved=WINDOW,
    )
    low = call(low_body, SHAPE((PARTS, 16, 128), BF16), (packed, normed), "vv", 20)
    low = swap(low, TP)
    base, ups, out_down, out_up = call(
        base_body,
        (
            SHAPE((32, 384), F32),
            SHAPE((64, 384), BF16),
            SHAPE((64, 256), BF16),
            SHAPE((64, 384), BF16),
        ),
        (packed, normed, query_matrix, key_matrix.T, value_matrix.T),
        "vvaaa",
        12,
        [
            pltpu.VMEM(query_matrix.shape, BF16),
            pltpu.VMEM((32, width), BF16),
            pltpu.VMEM((32, width), BF16),
            dma((CHUNKS + 2,)),
        ],
        moved=WINDOW,
    )
    queries, own, fresh = call(
        query_body,
        (SHAPE((PARTS, 64, 128), BF16), SHAPE((64, 128), BF16), SHAPE((16, 128), BF16)),
        (low, base, ups, cosines, sines, query_norm_gain),
        "vvvvvv",
        20,
    )
    gathered = swap(queries, TP)
    fresh = [fresh] + [
        lax.ppermute(fresh, "near", [(i, i ^ k) for i in range(4)]) for k in range(1, 4)
    ]
    parts = call(
        attend_body,
        SHAPE((PARTS, 72, 128), BF16),
        (place, filled_lengths, gathered, stored_keys, stored_values),
        "ssvvv",
        20,
    )
    parts = swap(parts, TP)
    own_weighted, own_stats = call(
        fresh_body,
        (SHAPE((64, 128), F32), SHAPE((8, 128), F32)),
        (place, *fresh, own, cosines, sines, key_norm_gain),
        "svvvvvvvv",
        20,
        [pltpu.VMEM((4, 16, 128), F32)],
        moved=WINDOW,
    )
    partial = call(
        output_body,
        SHAPE((PARTS, 32, 384), BF16),
        (parts, own_weighted, own_stats, output_matrix, out_down),
        "vvvav",
        12,
        [pltpu.VMEM(output_matrix.shape, BF16), dma((CHUNKS,))],
    )
    partial = swap(partial, TP)
    return call(finish_body, SHAPE((ROWS, TOKENS, 320), BF16), (partial, out_up), "vv", 20)


def solution(mesh):
    fine = Mesh(mesh.devices.reshape(16, 4, 4), ("group", "far", "near"))
    group, tp = "group", TP
    in_specs = (
        P(group, None, None),
        P(),
        P(),
        P(),
        P(None, tp),
        P(None, tp),
        P(None, tp),
        P(tp, None),
        P(group, tp),
        P(group, tp),
        P(group, tp),
        P(group, tp),
        P(tp, group),
        P(group, tp),
        P(group, tp, None),
        P(group, tp, None),
        P(group),
    )
    out_specs = P(group, None, tp)
    return jax.shard_map(local, mesh=fine, in_specs=in_specs, out_specs=out_specs, check_vma=False)
```

```python
import functools
import math

import jax
import jax.numpy as jnp
import numpy as np
from jax import lax
from jax.experimental import pallas as pl
from jax.experimental.pallas import tpu as pltpu
from jax.sharding import Mesh
from jax.sharding import PartitionSpec as P

EPS = 1e-06
ADAPTER_SCALE = 2.0
THETA = 1000000.0
GROUPS = 16
PARTS = 16
TP = ("far", "near")
HEAD = 128
TOKENS = 4
ROWS = 8
F32 = jnp.float32
BF16 = jnp.bfloat16
SHAPE = jax.ShapeDtypeStruct
WINDOW = 16 * 2**20


def call(body, out_shapes, args, spaces, room, scratch=(), left=(), moved=0):
    places = {"s": pltpu.SMEM, "a": pltpu.HBM, "v": pltpu.VMEM}
    specs = [pl.BlockSpec(memory_space=places[c]) for c in spaces]
    many = isinstance(out_shapes, tuple)
    outs = [
        pl.BlockSpec(memory_space=pltpu.HBM if i in left else pltpu.VMEM)
        for i in range(len(out_shapes) if many else 1)
    ]
    return pl.pallas_call(
        body,
        out_shape=out_shapes,
        in_specs=specs,
        out_specs=tuple(outs) if many else outs[0],
        scratch_shapes=list(scratch),
        compiler_params=pltpu.CompilerParams(vmem_limit_bytes=int((64 - room) * 2**20)),
        cost_estimate=pl.CostEstimate(flops=0, bytes_accessed=moved, transcendentals=0),
    )(*args)


def dot(a, b, contract=(1, 0)):
    return lax.dot_general(
        a, b, (((contract[0],), (contract[1],)), ((), ())), preferred_element_type=F32
    )


def widen(block, lanes):
    return jnp.concatenate(
        [block, jnp.zeros((block.shape[0], lanes - block.shape[1]), block.dtype)], axis=1
    )


def iotas(shape):
    return [lax.broadcasted_iota(jnp.int32, shape, d) for d in range(2)]


def fetch(sources, held, sems):
    copies = [pltpu.make_async_copy(s, h, sems.at[i]) for i, (s, h) in enumerate(zip(sources, held))]
    for copy in copies:
        copy.start()
    return copies


def pack_body(*refs):
    packed, held = refs[6], refs[7:13]
    for copy in fetch(refs[:6], held, refs[13]):
        copy.wait()
    down, out_down, query_up, key_up, value_up, out_up = [h[...].astype(F32) for h in held]
    up = jnp.concatenate([query_up, key_up, value_up], axis=1)
    block = jnp.concatenate(
        [widen(down, 384), widen(out_down, 384), widen(up, 384), widen(out_up, 384)], axis=0
    ).astype(BF16)
    for i in range(GROUPS):
        packed[i] = block


CHUNKS = 4


def prepare_body(
    lengths, x_any, gain_any, inverse_any, query_any, key_any, value_any,
    normed, cosines, sines, base, x_ref, gain, inverse, query_w, key_w, value_w, sems,
):
    step = query_any.shape[0] // CHUNKS
    rows = [pl.ds(c * step, step) for c in range(CHUNKS)]
    copies = fetch(
        [x_any, gain_any, inverse_any, key_any, value_any] + [query_any.at[r] for r in rows],
        [x_ref, gain, inverse, key_w, value_w] + [query_w.at[r] for r in rows],
        sems,
    )
    for copy in copies[:3]:
        copy.wait()
    x = x_ref[...].astype(F32).reshape(ROWS * TOKENS, -1)
    scale = lax.rsqrt(jnp.mean(x * x, axis=-1, keepdims=True) + EPS)
    value = (x * scale * gain[...].astype(F32).reshape(1, -1)).astype(BF16)
    normed[...] = value
    row, lane = iotas((ROWS * TOKENS, HEAD))
    position = row % TOKENS
    for b in range(ROWS):
        position = position + jnp.where(row // TOKENS == b, lengths[b], 0)
    angles = position.astype(F32) * inverse[...]
    cosines[...] = jnp.cos(angles)
    sines[...] = jnp.where(lane < 64, -1.0, 1.0) * jnp.sin(angles)
    copies[3].wait()
    copies[4].wait()
    both = jnp.concatenate([key_w[...], value_w[...]], axis=0)
    base[:, 256:384] = widen(dot(value, both, (1, 1)), 128)
    raw = jnp.zeros((32, 256), F32)
    for c in range(CHUNKS):
        copies[5 + c].wait()
        part = slice(c * step, (c + 1) * step)
        raw = raw + dot(value[:, part], query_w[part, :])
    base[:, 0:256] = raw


def low_body(packed, normed, low):
    pieces = [packed[g, 0:16, 0:320].astype(F32) for g in range(GROUPS)]
    down = jnp.concatenate(pieces, axis=1).astype(BF16)
    block = widen(dot(down, normed[...], (1, 1)), 128).astype(BF16)
    for t in range(PARTS):
        low[t] = block


def unpack_body(packed, ups, out_down, out_up):
    pieces = [packed[g].astype(F32) for g in range(GROUPS)]
    out_down[...] = jnp.concatenate([p[12:16, 0:256] for p in pieces], axis=0).astype(BF16)
    ups[...] = jnp.concatenate([p[16:20] for p in pieces], axis=0).astype(BF16)
    out_up[...] = jnp.concatenate([p[20:24] for p in pieces], axis=0).astype(BF16)


def rms_rope(heads, gain, cosines, sines):
    scale = lax.rsqrt(jnp.mean(heads * heads, axis=-1, keepdims=True) + EPS)
    heads = heads * scale * gain
    return heads * cosines + pltpu.roll(heads, 64, 1) * sines


def regroup(count_from, count_to):
    row, col = iotas((64, 64))
    source = ((row // TOKENS) % count_to) * (count_from * TOKENS)
    source = source + (row // (TOKENS * count_to)) * TOKENS + row % TOKENS
    return jnp.where(col == source, 1.0, 0.0).astype(BF16)


def query_body(low, base, ups, cosines, sines, gain, packed, own, fresh):
    ranks = jnp.concatenate([low[t].astype(F32)[0:12] for t in range(PARTS)], axis=0)
    ranks = ranks[:, 0:32].astype(BF16)
    lift = ups[...]
    _, column = iotas(lift.shape)
    zero = jnp.zeros_like(lift)
    lifts = [
        jnp.where((column >= first) & (column < last), lift, zero)
        for first, last in ((0, 256), (256, 288), (288, 320))
    ]
    update = dot(ranks, jnp.concatenate(lifts, axis=0), (0, 0))
    raw = base[...] + ADAPTER_SCALE * update
    scale = gain[...].astype(F32).reshape(1, -1)
    heads = [
        rms_rope(raw[:, j * HEAD : (j + 1) * HEAD], scale, cosines[...], sines[...])
        for j in range(2)
    ]
    queries = jnp.concatenate(heads, axis=0).astype(BF16)
    queries = dot(regroup(8, 2), queries).astype(BF16)
    for i in range(PARTS):
        packed[i] = queries
    own[...] = queries
    _, lane = iotas((16, 128))
    folded = jnp.where(lane < 64, raw[0:16, 256:384], pltpu.roll(raw[16:32, 256:384], 64, 1))
    fresh[...] = folded.astype(BF16)


def softmax_parts(scores, usable):
    masked = jnp.where(usable, scores, -1e30)
    highest = jnp.maximum(jnp.max(masked, axis=-1, keepdims=True), -1e29)
    highest = highest.astype(BF16).astype(F32)
    weights = jnp.exp(masked - highest).astype(BF16)
    total = jnp.sum(weights.astype(F32), axis=-1, keepdims=True)
    return highest, weights, total


SCALING = 1.0 / math.sqrt(HEAD)
SPAN = 128


def attend_body(place, lengths, gathered, keys, values, packed):
    offset = place[0] * SPAN
    everything = [gathered[t].astype(F32) for t in range(PARTS)]
    _, lane = iotas((128, 128))
    stats = jnp.zeros((128, 128), F32)
    empty = jnp.zeros((32, 128), BF16)
    found = []
    for b in range(ROWS):
        query = jnp.concatenate(
            [q[b * 8 : (b + 1) * 8] for q in everything], axis=0
        ).astype(BF16)
        query = jnp.concatenate(
            [
                jnp.concatenate(
                    [query[n * 32 : (n + 1) * 32] if m == n else empty for m in range(4)], axis=1
                )
                for n in range(4)
            ],
            axis=0,
        )
        scores = dot(query, keys[b], (1, 1))
        highest, weights, total = softmax_parts(scores * SCALING, lane + offset < lengths[b])
        total_high = total.astype(BF16).astype(F32)
        stats = jnp.where(lane == b, highest, stats)
        stats = jnp.where(lane == 8 + b, total_high, stats)
        stats = jnp.where(lane == 16 + b, total - total_high, stats)
        weighted = dot(weights, values[b])
        found.append(
            [weighted[n * 32 : (n + 1) * 32, n * HEAD : (n + 1) * HEAD] for n in range(4)]
        )
    for t in range(PARTS):
        rows = slice(t % 4 * 8, t % 4 * 8 + 8)
        block = [found[b][t // 4][rows] for b in range(ROWS)] + [stats[t * 8 : (t + 1) * 8]]
        packed[t] = jnp.concatenate(block, axis=0).astype(BF16)


def fresh_body(
    place, near, near_1, near_2, near_3, own, cosines, sines, gain, weighted, stats_out, gathered
):
    for k, piece in enumerate((near, near_1, near_2, near_3)):
        gathered[(place[0] % 4) ^ k] = piece[...].astype(F32)
    fresh_key = []
    fresh_value = []
    for q in range(4):
        fold = gathered[q]
        wide = jnp.concatenate([fold, pltpu.roll(fold, 64, 1)], axis=0)
        fresh_key.append(wide[:, 0:32])
        fresh_value.append(wide[:, 32:64])
    new_keys = jnp.concatenate(fresh_key, axis=1)
    scale = gain[...].astype(F32).reshape(1, -1)
    new_keys = rms_rope(new_keys, scale, cosines[...], sines[...]).astype(BF16)
    new_values = jnp.concatenate(fresh_value, axis=1).astype(BF16)
    scores = dot(own[...], new_keys, (1, 1)) * SCALING
    row, col = iotas((64, 32))
    usable = (row // 8 == col // TOKENS) & (col % TOKENS <= row % TOKENS)
    highest, weights, total = softmax_parts(scores, usable)
    weighted[...] = dot(weights, new_values)
    _, lane = iotas((8, 128))
    stats = jnp.zeros((8, 128), F32)
    for b in range(ROWS):
        stats = jnp.where(lane == b, highest[b * 8 : (b + 1) * 8], stats)
        stats = jnp.where(lane == 8 + b, total[b * 8 : (b + 1) * 8], stats)
    stats_out[...] = stats


def load_body(source, held, sem):
    copy = pltpu.make_async_copy(source, held, sem)
    copy.start()
    copy.wait()


def output_body(
    gathered, own_weighted, own_stats, output_w, out_down, packed
):
    blocks = [gathered[t].astype(F32) for t in range(PARTS)]
    stats = [block[64:72] for block in blocks] + [own_stats[...]]
    values = [block[0:64] for block in blocks] + [own_weighted[...]]
    highest = functools.reduce(jnp.maximum, stats)
    factors = [jnp.exp(jnp.minimum(s - highest, 0.0)) for s in stats]
    total = jnp.zeros((8, 128), F32)
    for s, f in zip(stats, factors):
        total = total + f * (pltpu.roll(s, 120, 1) + pltpu.roll(s, 112, 1))
    _, lane = iotas((8, 128))
    inverse = 1.0 / jnp.where(lane < 8, total, 1.0)
    pieces = []
    for b in range(ROWS):
        piece = jnp.zeros((8, 128), F32)
        for v, f in zip(values, factors):
            piece = piece + f[:, b : b + 1] * v[b * 8 : (b + 1) * 8]
        pieces.append(piece * inverse[:, b : b + 1])
    heads = jnp.concatenate(pieces, axis=0).astype(BF16)
    heads = dot(regroup(2, 8), heads).astype(BF16)
    heads = jnp.concatenate([heads[0:32], heads[32:64]], axis=1)
    low = dot(heads, out_down[...], (1, 1))
    partial = dot(heads, output_w[...])
    for t in range(PARTS):
        block = jnp.concatenate([partial[:, t * 320 : (t + 1) * 320], low], axis=1)
        packed[t] = block.astype(BF16)


def finish_body(gathered, out_up, result):
    total = gathered[0].astype(F32)
    for t in range(1, PARTS):
        total = total + gathered[t].astype(F32)
    update = dot(total[:, 320:384].astype(BF16), out_up[...])
    out = total[:, 0:320] + ADAPTER_SCALE * update[:, 0:320]
    result[...] = out.reshape(ROWS, TOKENS, 320).astype(BF16)


def swap(block, axis):
    return lax.all_to_all(block, axis, 0, 0)


def local(
    layer_inputs,
    input_norm_gain,
    query_norm_gain,
    key_norm_gain,
    query_matrix,
    key_matrix,
    value_matrix,
    output_matrix,
    adapter_down,
    query_up_factor,
    key_up_factor,
    value_up_factor,
    output_down_factor,
    output_up_factor,
    stored_keys,
    stored_values,
    filled_lengths,
):
    dma = pltpu.SemaphoreType.DMA
    width = layer_inputs.shape[-1]
    place = lax.axis_index(TP).astype(jnp.int32).reshape(1)
    shards = (
        adapter_down.T,
        output_down_factor.T,
        query_up_factor,
        key_up_factor,
        value_up_factor,
        output_up_factor,
    )
    packed = call(
        pack_body,
        SHAPE((GROUPS, 24, 384), BF16),
        shards,
        "aaaaaa",
        8,
        [pltpu.VMEM(s.shape, BF16) for s in shards] + [dma((6,))],
    )
    packed = swap(packed, "group")

    inverse = THETA ** (-(np.arange(64, dtype=np.float64) * 2.0 / HEAD))
    inverse = jnp.asarray(np.concatenate([inverse, inverse]).reshape(1, HEAD), F32)
    normed, cosines, sines, base = call(
        prepare_body,
        (
            SHAPE((32, width), BF16),
            SHAPE((32, HEAD), F32),
            SHAPE((32, HEAD), F32),
            SHAPE((32, 384), F32),
        ),
        (
            filled_lengths,
            layer_inputs,
            input_norm_gain,
            inverse,
            query_matrix,
            key_matrix.T,
            value_matrix.T,
        ),
        "saaaaaa",
        10.75,
        [
            pltpu.VMEM(layer_inputs.shape, BF16),
            pltpu.VMEM((width,), BF16),
            pltpu.VMEM((1, HEAD), F32),
            pltpu.VMEM(query_matrix.shape, BF16),
            pltpu.VMEM((32, width), BF16),
            pltpu.VMEM((32, width), BF16),
            dma((5 + CHUNKS,)),
        ],
        moved=WINDOW,
    )
    low = call(low_body, SHAPE((PARTS, 16, 128), BF16), (packed, normed), "vv", 20)
    low = swap(low, TP)
    ups, out_down, out_up = call(
        unpack_body,
        (SHAPE((64, 384), BF16), SHAPE((64, 256), BF16), SHAPE((64, 384), BF16)),
        (packed,),
        "v",
        20,
        moved=WINDOW,
    )
    queries, own, fresh = call(
        query_body,
        (SHAPE((PARTS, 64, 128), BF16), SHAPE((64, 128), BF16), SHAPE((16, 128), BF16)),
        (low, base, ups, cosines, sines, query_norm_gain),
        "vvvvvv",
        20,
    )
    gathered = swap(queries, TP)
    fresh = [fresh] + [
        lax.ppermute(fresh, "near", [(i, i ^ k) for i in range(4)]) for k in range(1, 4)
    ]
    own_weighted, own_stats = call(
        fresh_body,
        (SHAPE((64, 128), F32), SHAPE((8, 128), F32)),
        (place, *fresh, own, cosines, sines, key_norm_gain),
        "svvvvvvvv",
        20,
        [pltpu.VMEM((4, 16, 128), F32)],
        moved=WINDOW,
    )
    gathered, own_weighted, own_stats = lax.optimization_barrier(
        (gathered, own_weighted, own_stats)
    )
    parts = call(
        attend_body,
        SHAPE((PARTS, 72, 128), BF16),
        (place, filled_lengths, gathered, stored_keys, stored_values),
        "ssvvv",
        20,
    )
    parts, output_late = lax.optimization_barrier((parts, output_matrix))
    parts = swap(parts, TP)
    output_late = call(
        load_body, SHAPE(output_matrix.shape, BF16), (output_late,), "a", 14, [dma], moved=WINDOW
    )
    partial = call(
        output_body,
        SHAPE((PARTS, 32, 384), BF16),
        (parts, own_weighted, own_stats, output_late, out_down),
        "vvvvv",
        20,
    )
    partial = swap(partial, TP)
    return call(finish_body, SHAPE((ROWS, TOKENS, 320), BF16), (partial, out_up), "vv", 20)


def solution(mesh):
    fine = Mesh(mesh.devices.reshape(16, 4, 4), ("group", "far", "near"))
    group, tp = "group", TP
    in_specs = (
        P(group, None, None),
        P(),
        P(),
        P(),
        P(None, tp),
        P(None, tp),
        P(None, tp),
        P(tp, None),
        P(group, tp),
        P(group, tp),
        P(group, tp),
        P(group, tp),
        P(tp, group),
        P(group, tp),
        P(group, tp, None),
        P(group, tp, None),
        P(group),
    )
    out_specs = P(group, None, tp)
    return jax.shard_map(local, mesh=fine, in_specs=in_specs, out_specs=out_specs, check_vma=False)
```

```python
import functools
import math

import jax
import jax.numpy as jnp
import numpy as np
from jax import lax
from jax.experimental import pallas as pl
from jax.experimental.pallas import tpu as pltpu
from jax.sharding import PartitionSpec as P

EPS = 1e-06
ADAPTER_SCALE = 2.0
THETA = 1000000.0
GROUPS = 16
PARTS = 16
HEAD = 128
TOKENS = 4
ROWS = 8
F32 = jnp.float32
BF16 = jnp.bfloat16
SHAPE = jax.ShapeDtypeStruct
WINDOW = 16 * 2**20


def call(body, out_shapes, args, spaces, room, scratch=(), left=(), moved=0):
    places = {"s": pltpu.SMEM, "a": pltpu.HBM, "v": pltpu.VMEM}
    specs = [pl.BlockSpec(memory_space=places[c]) for c in spaces]
    many = isinstance(out_shapes, tuple)
    outs = [
        pl.BlockSpec(memory_space=pltpu.HBM if i in left else pltpu.VMEM)
        for i in range(len(out_shapes) if many else 1)
    ]
    return pl.pallas_call(
        body,
        out_shape=out_shapes,
        in_specs=specs,
        out_specs=tuple(outs) if many else outs[0],
        scratch_shapes=list(scratch),
        compiler_params=pltpu.CompilerParams(vmem_limit_bytes=int((64 - room) * 2**20)),
        cost_estimate=pl.CostEstimate(flops=0, bytes_accessed=moved, transcendentals=0),
    )(*args)


def dot(a, b, contract=(1, 0)):
    return lax.dot_general(
        a, b, (((contract[0],), (contract[1],)), ((), ())), preferred_element_type=F32
    )


def widen(block, lanes):
    return jnp.concatenate(
        [block, jnp.zeros((block.shape[0], lanes - block.shape[1]), block.dtype)], axis=1
    )


def iotas(shape):
    return [lax.broadcasted_iota(jnp.int32, shape, d) for d in range(2)]


def fetch(sources, held, sems):
    copies = [pltpu.make_async_copy(s, h, sems.at[i]) for i, (s, h) in enumerate(zip(sources, held))]
    for copy in copies:
        copy.start()
    return copies


def pack_body(*refs):
    packed, held = refs[6], refs[7:13]
    for copy in fetch(refs[:6], held, refs[13]):
        copy.wait()
    down, out_down, query_up, key_up, value_up, out_up = [h[...].astype(F32) for h in held]
    up = jnp.concatenate([query_up, key_up, value_up], axis=1)
    block = jnp.concatenate(
        [widen(down, 384), widen(out_down, 384), widen(up, 384), widen(out_up, 384)], axis=0
    ).astype(BF16)
    for i in range(GROUPS):
        packed[i] = block


CHUNKS = 4


def prepare_body(
    lengths, x_any, gain_any, inverse_any, query_any, key_any, value_any,
    normed, cosines, sines, base, fresh, x_ref, gain, inverse, query_w, key_w, value_w, sems,
):
    step = query_any.shape[0] // CHUNKS
    rows = [pl.ds(c * step, step) for c in range(CHUNKS)]
    copies = fetch(
        [x_any, gain_any, inverse_any, key_any, value_any] + [query_any.at[r] for r in rows],
        [x_ref, gain, inverse, key_w, value_w] + [query_w.at[r] for r in rows],
        sems,
    )
    for copy in copies[:3]:
        copy.wait()
    x = x_ref[...].astype(F32).reshape(ROWS * TOKENS, -1)
    scale = lax.rsqrt(jnp.mean(x * x, axis=-1, keepdims=True) + EPS)
    value = (x * scale * gain[...].astype(F32).reshape(1, -1)).astype(BF16)
    normed[...] = value
    row, lane = iotas((ROWS * TOKENS, HEAD))
    position = row % TOKENS
    for b in range(ROWS):
        position = position + jnp.where(row // TOKENS == b, lengths[b], 0)
    angles = position.astype(F32) * inverse[...]
    cosines[...] = jnp.cos(angles)
    sines[...] = jnp.where(lane < 64, -1.0, 1.0) * jnp.sin(angles)
    copies[3].wait()
    copies[4].wait()
    both = jnp.concatenate([key_w[...], value_w[...]], axis=0)
    fresh[...] = widen(dot(value, both, (1, 1)), 128)
    raw = jnp.zeros((32, 256), F32)
    for c in range(CHUNKS):
        copies[5 + c].wait()
        part = slice(c * step, (c + 1) * step)
        raw = raw + dot(value[:, part], query_w[part, :])
    base[...] = raw


def fold(block):
    rows = block.shape[0] // 2
    _, lane = iotas((rows, 128))
    return jnp.where(lane < 64, block[0:rows], pltpu.roll(block[rows:], 64, 1))


def unfold(block):
    return jnp.concatenate([block, pltpu.roll(block, 64, 1)], axis=0)


def low_body(packed, normed, fresh, low, near):
    pieces = [packed[g].astype(F32) for g in range(GROUPS)]
    down = jnp.concatenate([p[0:16, 0:320] for p in pieces], axis=1).astype(BF16)
    block = widen(dot(down, normed[...], (1, 1)), 128).astype(BF16)
    for t in range(PARTS):
        low[t] = block
    lift = jnp.concatenate([p[16:20, 256:384] for p in pieces], axis=0)
    near[0:16] = fold(fresh[...]).astype(BF16)
    near[16:48] = fold(lift).astype(BF16)


def unpack_body(packed, ups, out_down, out_up):
    pieces = [packed[g].astype(F32) for g in range(GROUPS)]
    out_down[...] = jnp.concatenate([p[12:16, 0:256] for p in pieces], axis=0).astype(BF16)
    lift = jnp.concatenate([p[16:20, 0:256] for p in pieces], axis=0)
    lift = jnp.concatenate([lift, jnp.zeros((8, 256), F32)], axis=0)
    rest = jnp.zeros((4, 256), F32)
    for t in range(6):
        block = jnp.concatenate([lift[t * 12 : (t + 1) * 12], rest], axis=0)
        ups[t * 16 : (t + 1) * 16] = block.astype(BF16)
    out_up[...] = jnp.concatenate([p[20:24] for p in pieces], axis=0).astype(BF16)


def rms_rope(heads, gain, cosines, sines):
    scale = lax.rsqrt(jnp.mean(heads * heads, axis=-1, keepdims=True) + EPS)
    heads = heads * scale * gain
    return heads * cosines + pltpu.roll(heads, 64, 1) * sines


def regroup(count_from, count_to):
    row, col = iotas((64, 64))
    source = ((row // TOKENS) % count_to) * (count_from * TOKENS)
    source = source + (row // (TOKENS * count_to)) * TOKENS + row % TOKENS
    return jnp.where(col == source, 1.0, 0.0).astype(BF16)


def query_body(low, base, ups, cosines, sines, gain, packed, own):
    ranks = low[0:6].reshape(96, 128)[:, 0:32]
    update = dot(ranks, ups[...], (0, 0))
    raw = base[...] + ADAPTER_SCALE * update
    scale = gain[...].astype(F32).reshape(1, -1)
    heads = [
        rms_rope(raw[:, j * HEAD : (j + 1) * HEAD], scale, cosines[...], sines[...])
        for j in range(2)
    ]
    queries = jnp.concatenate(heads, axis=0).astype(BF16)
    queries = dot(regroup(8, 2), queries).astype(BF16)
    for i in range(PARTS):
        packed[i] = queries
    own[...] = queries


def softmax_parts(scores, usable):
    masked = jnp.where(usable, scores, -1e30)
    highest = jnp.maximum(jnp.max(masked, axis=-1, keepdims=True), -1e29)
    highest = highest.astype(BF16).astype(F32)
    weights = jnp.exp(masked - highest).astype(BF16)
    total = jnp.sum(weights.astype(F32), axis=-1, keepdims=True)
    return highest, weights, total


SCALING = 1.0 / math.sqrt(HEAD)
SPAN = 128


def attend_body(place, lengths, gathered, keys, values, packed):
    offset = place[0] * SPAN
    everything = [gathered[t].astype(F32) for t in range(PARTS)]
    _, lane = iotas((128, 128))
    stats = jnp.zeros((128, 128), F32)
    empty = jnp.zeros((32, 128), BF16)
    found = []
    for b in range(ROWS):
        query = jnp.concatenate(
            [q[b * 8 : (b + 1) * 8] for q in everything], axis=0
        ).astype(BF16)
        query = jnp.concatenate(
            [
                jnp.concatenate(
                    [query[n * 32 : (n + 1) * 32] if m == n else empty for m in range(4)], axis=1
                )
                for n in range(4)
            ],
            axis=0,
        )
        scores = dot(query, keys[b], (1, 1))
        highest, weights, total = softmax_parts(scores * SCALING, lane + offset < lengths[b])
        total_high = total.astype(BF16).astype(F32)
        stats = jnp.where(lane == b, highest, stats)
        stats = jnp.where(lane == 8 + b, total_high, stats)
        stats = jnp.where(lane == 16 + b, total - total_high, stats)
        weighted = dot(weights, values[b])
        found.append(
            [weighted[n * 32 : (n + 1) * 32, n * HEAD : (n + 1) * HEAD] for n in range(4)]
        )
    for t in range(PARTS):
        rows = slice(t % 4 * 8, t % 4 * 8 + 8)
        block = [found[b][t // 4][rows] for b in range(ROWS)] + [stats[t * 8 : (t + 1) * 8]]
        packed[t] = jnp.concatenate(block, axis=0).astype(BF16)


def fresh_body(
    place, near, near_1, near_2, near_3, low, own, cosines, sines, gain,
    weighted, stats_out, pieces,
):
    for k, piece in enumerate((near, near_1, near_2, near_3)):
        pieces[(place[0] % 4) ^ k] = piece[...]
    ranks = [low[t].astype(F32)[0:12] for t in range(PARTS)]
    ranks = jnp.concatenate(ranks, axis=0)[:, 0:32].astype(BF16)
    fresh_key = []
    fresh_value = []
    for q in range(4):
        raw = unfold(pieces[q, 0:16].astype(F32))
        lift = unfold(pieces[q, 16:48].astype(F32)).astype(BF16)
        key = raw + ADAPTER_SCALE * dot(ranks[64:128], lift, (0, 0))
        value = raw + ADAPTER_SCALE * dot(ranks[128:192], lift, (0, 0))
        fresh_key.append(key[:, 0:32])
        fresh_value.append(value[:, 32:64])
    new_keys = jnp.concatenate(fresh_key, axis=1).astype(BF16).astype(F32)
    scale = gain[...].astype(F32).reshape(1, -1)
    new_keys = rms_rope(new_keys, scale, cosines[...], sines[...]).astype(BF16)
    new_values = jnp.concatenate(fresh_value, axis=1).astype(BF16)
    scores = dot(own[...], new_keys, (1, 1)) * SCALING
    row, col = iotas((64, 32))
    usable = (row // 8 == col // TOKENS) & (col % TOKENS <= row % TOKENS)
    highest, weights, total = softmax_parts(scores, usable)
    weighted[...] = dot(weights, new_values)
    _, lane = iotas((8, 128))
    stats = jnp.zeros((8, 128), F32)
    for b in range(ROWS):
        stats = jnp.where(lane == b, highest[b * 8 : (b + 1) * 8], stats)
        stats = jnp.where(lane == 8 + b, total[b * 8 : (b + 1) * 8], stats)
    stats_out[...] = stats


def load_body(source, held, sem):
    copy = pltpu.make_async_copy(source, held, sem)
    copy.start()
    copy.wait()


def output_body(
    gathered, own_weighted, own_stats, output_w, out_down, packed
):
    blocks = [gathered[t].astype(F32) for t in range(PARTS)]
    stats = [block[64:72] for block in blocks] + [own_stats[...]]
    values = [block[0:64] for block in blocks] + [own_weighted[...]]
    highest = functools.reduce(jnp.maximum, stats)
    factors = [jnp.exp(jnp.minimum(s - highest, 0.0)) for s in stats]
    total = jnp.zeros((8, 128), F32)
    for s, f in zip(stats, factors):
        total = total + f * (pltpu.roll(s, 120, 1) + pltpu.roll(s, 112, 1))
    _, lane = iotas((8, 128))
    inverse = 1.0 / jnp.where(lane < 8, total, 1.0)
    pieces = []
    for b in range(ROWS):
        piece = jnp.zeros((8, 128), F32)
        for v, f in zip(values, factors):
            piece = piece + f[:, b : b + 1] * v[b * 8 : (b + 1) * 8]
        pieces.append(piece * inverse[:, b : b + 1])
    heads = jnp.concatenate(pieces, axis=0).astype(BF16)
    heads = dot(regroup(2, 8), heads).astype(BF16)
    heads = jnp.concatenate([heads[0:32], heads[32:64]], axis=1)
    low = dot(heads, out_down[...], (1, 1))
    partial = dot(heads, output_w[...])
    for t in range(PARTS):
        block = jnp.concatenate([partial[:, t * 320 : (t + 1) * 320], low], axis=1)
        packed[t] = block.astype(BF16)


def finish_body(gathered, out_up, result):
    total = gathered[0].astype(F32)
    for t in range(1, PARTS):
        total = total + gathered[t].astype(F32)
    update = dot(total[:, 320:384].astype(BF16), out_up[...])
    out = total[:, 0:320] + ADAPTER_SCALE * update[:, 0:320]
    result[...] = out.reshape(ROWS, TOKENS, 320).astype(BF16)


def swap(block, axis):
    return lax.all_to_all(block, axis, 0, 0)


def local(
    layer_inputs,
    input_norm_gain,
    query_norm_gain,
    key_norm_gain,
    query_matrix,
    key_matrix,
    value_matrix,
    output_matrix,
    adapter_down,
    query_up_factor,
    key_up_factor,
    value_up_factor,
    output_down_factor,
    output_up_factor,
    stored_keys,
    stored_values,
    filled_lengths,
):
    dma = pltpu.SemaphoreType.DMA
    width = layer_inputs.shape[-1]
    place = lax.axis_index("tp").astype(jnp.int32).reshape(1)
    shards = (
        adapter_down.T,
        output_down_factor.T,
        query_up_factor,
        key_up_factor,
        value_up_factor,
        output_up_factor,
    )
    packed = call(
        pack_body,
        SHAPE((GROUPS, 24, 384), BF16),
        shards,
        "aaaaaa",
        8,
        [pltpu.VMEM(s.shape, BF16) for s in shards] + [dma((6,))],
    )
    packed, place = lax.optimization_barrier((packed, place))
    packed = swap(packed, "group")

    inverse = THETA ** (-(np.arange(64, dtype=np.float64) * 2.0 / HEAD))
    inverse = jnp.asarray(np.concatenate([inverse, inverse]).reshape(1, HEAD), F32)
    normed, cosines, sines, base, fresh = call(
        prepare_body,
        (
            SHAPE((32, width), BF16),
            SHAPE((32, HEAD), F32),
            SHAPE((32, HEAD), F32),
            SHAPE((32, 256), F32),
            SHAPE((32, HEAD), F32),
        ),
        (
            filled_lengths,
            layer_inputs,
            input_norm_gain,
            inverse,
            query_matrix,
            key_matrix.T,
            value_matrix.T,
        ),
        "saaaaaa",
        10.75,
        [
            pltpu.VMEM(layer_inputs.shape, BF16),
            pltpu.VMEM((width,), BF16),
            pltpu.VMEM((1, HEAD), F32),
            pltpu.VMEM(query_matrix.shape, BF16),
            pltpu.VMEM((32, width), BF16),
            pltpu.VMEM((32, width), BF16),
            dma((5 + CHUNKS,)),
        ],
        moved=WINDOW,
    )
    low, near = call(
        low_body,
        (SHAPE((PARTS, 16, 128), BF16), SHAPE((48, 128), BF16)),
        (packed, normed, fresh),
        "vvv",
        20,
    )
    low = swap(low, "tp")
    near = [near] + [
        lax.ppermute(near, "tp", [(i, i ^ k) for i in range(PARTS)]) for k in range(1, 4)
    ]
    ups, out_down, out_up = call(
        unpack_body,
        (SHAPE((96, 256), BF16), SHAPE((64, 256), BF16), SHAPE((64, 384), BF16)),
        (packed,),
        "v",
        20,
        moved=WINDOW,
    )
    low, near = lax.optimization_barrier((low, near))
    queries, own = call(
        query_body,
        (SHAPE((PARTS, 64, 128), BF16), SHAPE((64, 128), BF16)),
        (low, base, ups, cosines, sines, query_norm_gain),
        "vvvvvv",
        20,
    )
    gathered = swap(queries, "tp")
    parts = call(
        attend_body,
        SHAPE((PARTS, 72, 128), BF16),
        (place, filled_lengths, gathered, stored_keys, stored_values),
        "ssvvv",
        20,
    )
    parts, own, output_late = lax.optimization_barrier((parts, own, output_matrix))
    parts = swap(parts, "tp")
    output_late = call(
        load_body, SHAPE(output_matrix.shape, BF16), (output_late,), "a", 14, [dma], moved=WINDOW
    )
    own_weighted, own_stats = call(
        fresh_body,
        (SHAPE((64, 128), F32), SHAPE((8, 128), F32)),
        (place, *near, low, own, cosines, sines, key_norm_gain),
        "svvvvvvvvv",
        20,
        [pltpu.VMEM((4, 48, 128), BF16)],
        moved=WINDOW,
    )
    partial = call(
        output_body,
        SHAPE((PARTS, 32, 384), BF16),
        (parts, own_weighted, own_stats, output_late, out_down),
        "vvvvv",
        20,
    )
    partial = swap(partial, "tp")
    return call(finish_body, SHAPE((ROWS, TOKENS, 320), BF16), (partial, out_up), "vv", 20)


def solution(mesh):
    in_specs = (
        P("group", None, None),
        P(),
        P(),
        P(),
        P(None, "tp"),
        P(None, "tp"),
        P(None, "tp"),
        P("tp", None),
        P("group", "tp"),
        P("group", "tp"),
        P("group", "tp"),
        P("group", "tp"),
        P("tp", "group"),
        P("group", "tp"),
        P("group", "tp", None),
        P("group", "tp", None),
        P("group"),
    )
    out_specs = P("group", None, "tp")
    return jax.shard_map(local, mesh=mesh, in_specs=in_specs, out_specs=out_specs, check_vma=False)
```

```python
import functools
import math

import jax
import jax.numpy as jnp
import numpy as np
from jax import lax
from jax.experimental import pallas as pl
from jax.experimental.pallas import tpu as pltpu
from jax.sharding import PartitionSpec as P

EPS = 1e-06
ADAPTER_SCALE = 2.0
THETA = 1000000.0
GROUPS = 16
PARTS = 16
HEAD = 128
TOKENS = 4
ROWS = 8
F32 = jnp.float32
BF16 = jnp.bfloat16
SHAPE = jax.ShapeDtypeStruct
WINDOW = 16 * 2**20


def call(body, out_shapes, args, spaces, room, scratch=(), left=(), moved=0):
    places = {"s": pltpu.SMEM, "a": pltpu.HBM, "v": pltpu.VMEM}
    specs = [pl.BlockSpec(memory_space=places[c]) for c in spaces]
    many = isinstance(out_shapes, tuple)
    outs = [
        pl.BlockSpec(memory_space=pltpu.HBM if i in left else pltpu.VMEM)
        for i in range(len(out_shapes) if many else 1)
    ]
    return pl.pallas_call(
        body,
        out_shape=out_shapes,
        in_specs=specs,
        out_specs=tuple(outs) if many else outs[0],
        scratch_shapes=list(scratch),
        compiler_params=pltpu.CompilerParams(vmem_limit_bytes=int((64 - room) * 2**20)),
        cost_estimate=pl.CostEstimate(flops=0, bytes_accessed=moved, transcendentals=0),
    )(*args)


def dot(a, b, contract=(1, 0)):
    return lax.dot_general(
        a, b, (((contract[0],), (contract[1],)), ((), ())), preferred_element_type=F32
    )


def widen(block, lanes):
    return jnp.concatenate(
        [block, jnp.zeros((block.shape[0], lanes - block.shape[1]), block.dtype)], axis=1
    )


def iotas(shape):
    return [lax.broadcasted_iota(jnp.int32, shape, d) for d in range(2)]


def fetch(sources, held, sems):
    copies = [pltpu.make_async_copy(s, h, sems.at[i]) for i, (s, h) in enumerate(zip(sources, held))]
    for copy in copies:
        copy.start()
    return copies


def pack_body(*refs):
    packed, held = refs[6], refs[7:13]
    for copy in fetch(refs[:6], held, refs[13]):
        copy.wait()
    down, out_down, query_up, key_up, value_up, out_up = [h[...].astype(F32) for h in held]
    up = jnp.concatenate([query_up, key_up, value_up], axis=1)
    block = jnp.concatenate(
        [widen(down, 384), widen(out_down, 384), widen(up, 384), widen(out_up, 384)], axis=0
    ).astype(BF16)
    for i in range(GROUPS):
        packed[i] = block


CHUNKS = 4


def prepare_body(
    lengths, x_any, gain_any, inverse_any, query_any, key_any, value_any,
    normed, cosines, sines, base, fresh, x_ref, gain, inverse, query_w, key_w, value_w, sems,
):
    step = query_any.shape[0] // CHUNKS
    rows = [pl.ds(c * step, step) for c in range(CHUNKS)]
    copies = fetch(
        [x_any, gain_any, inverse_any, key_any, value_any] + [query_any.at[r] for r in rows],
        [x_ref, gain, inverse, key_w, value_w] + [query_w.at[r] for r in rows],
        sems,
    )
    for copy in copies[:3]:
        copy.wait()
    x = x_ref[...].astype(F32).reshape(ROWS * TOKENS, -1)
    scale = lax.rsqrt(jnp.mean(x * x, axis=-1, keepdims=True) + EPS)
    value = (x * scale * gain[...].astype(F32).reshape(1, -1)).astype(BF16)
    normed[...] = value
    row, lane = iotas((ROWS * TOKENS, HEAD))
    position = row % TOKENS
    for b in range(ROWS):
        position = position + jnp.where(row // TOKENS == b, lengths[b], 0)
    angles = position.astype(F32) * inverse[...]
    cosines[...] = jnp.cos(angles)
    sines[...] = jnp.where(lane < 64, -1.0, 1.0) * jnp.sin(angles)
    copies[3].wait()
    copies[4].wait()
    both = jnp.concatenate([key_w[...], value_w[...]], axis=0)
    fresh[...] = widen(dot(value, both, (1, 1)), 128)
    raw = jnp.zeros((32, 256), F32)
    for c in range(CHUNKS):
        copies[5 + c].wait()
        part = slice(c * step, (c + 1) * step)
        raw = raw + dot(value[:, part], query_w[part, :])
    base[...] = raw


def fold(block):
    rows = block.shape[0] // 2
    _, lane = iotas((rows, 128))
    return jnp.where(lane < 64, block[0:rows], pltpu.roll(block[rows:], 64, 1))


def unfold(block):
    return jnp.concatenate([block, pltpu.roll(block, 64, 1)], axis=0)


def low_body(packed, normed, fresh, low, near):
    pieces = [packed[g].astype(F32) for g in range(GROUPS)]
    down = jnp.concatenate([p[0:16, 0:320] for p in pieces], axis=1).astype(BF16)
    block = widen(dot(down, normed[...], (1, 1)), 128).astype(BF16)
    for t in range(PARTS):
        low[t] = block
    lift = jnp.concatenate([p[16:20, 256:384] for p in pieces], axis=0)
    near[0:16] = fold(fresh[...]).astype(BF16)
    near[16:48] = fold(lift).astype(BF16)


def unpack_body(packed, out_down, out_up):
    pieces = [packed[g].astype(F32) for g in range(GROUPS)]
    out_down[...] = jnp.concatenate([p[12:16, 0:256] for p in pieces], axis=0).astype(BF16)
    out_up[...] = jnp.concatenate([p[20:24] for p in pieces], axis=0).astype(BF16)


def rms_rope(heads, gain, cosines, sines):
    scale = lax.rsqrt(jnp.mean(heads * heads, axis=-1, keepdims=True) + EPS)
    heads = heads * scale * gain
    return heads * cosines + pltpu.roll(heads, 64, 1) * sines


def regroup(count_from, count_to):
    row, col = iotas((64, 64))
    source = ((row // TOKENS) % count_to) * (count_from * TOKENS)
    source = source + (row // (TOKENS * count_to)) * TOKENS + row % TOKENS
    return jnp.where(col == source, 1.0, 0.0).astype(BF16)


def query_body(low, packed, base, cosines, sines, gain, sent, own):
    ranks = jnp.concatenate([low[t].astype(F32)[0:12] for t in range(6)], axis=0)
    ranks = ranks[0:64, 0:32].astype(BF16)
    lift = [packed[g].astype(F32)[16:20, 0:256] for g in range(GROUPS)]
    update = dot(ranks, jnp.concatenate(lift, axis=0).astype(BF16), (0, 0))
    raw = base[...] + ADAPTER_SCALE * update
    scale = gain[...].astype(F32).reshape(1, -1)
    heads = [
        rms_rope(raw[:, j * HEAD : (j + 1) * HEAD], scale, cosines[...], sines[...])
        for j in range(2)
    ]
    queries = jnp.concatenate(heads, axis=0).astype(BF16)
    queries = dot(regroup(8, 2), queries).astype(BF16)
    for i in range(PARTS):
        sent[i] = queries
    own[...] = queries


def softmax_parts(scores, usable):
    masked = jnp.where(usable, scores, -1e30)
    highest = jnp.maximum(jnp.max(masked, axis=-1, keepdims=True), -1e29)
    highest = highest.astype(BF16).astype(F32)
    weights = jnp.exp(masked - highest).astype(BF16)
    total = jnp.sum(weights.astype(F32), axis=-1, keepdims=True)
    return highest, weights, total


SCALING = 1.0 / math.sqrt(HEAD)
SPAN = 128


def attend_body(place, lengths, gathered, keys, values, packed):
    offset = place[0] * SPAN
    everything = [gathered[t].astype(F32) for t in range(PARTS)]
    _, lane = iotas((128, 128))
    stats = jnp.zeros((128, 128), F32)
    empty = jnp.zeros((32, 128), BF16)
    found = []
    for b in range(ROWS):
        query = jnp.concatenate(
            [q[b * 8 : (b + 1) * 8] for q in everything], axis=0
        ).astype(BF16)
        query = jnp.concatenate(
            [
                jnp.concatenate(
                    [query[n * 32 : (n + 1) * 32] if m == n else empty for m in range(4)], axis=1
                )
                for n in range(4)
            ],
            axis=0,
        )
        scores = dot(query, keys[b], (1, 1))
        highest, weights, total = softmax_parts(scores * SCALING, lane + offset < lengths[b])
        total_high = total.astype(BF16).astype(F32)
        stats = jnp.where(lane == b, highest, stats)
        stats = jnp.where(lane == 8 + b, total_high, stats)
        stats = jnp.where(lane == 16 + b, total - total_high, stats)
        weighted = dot(weights, values[b])
        found.append(
            [weighted[n * 32 : (n + 1) * 32, n * HEAD : (n + 1) * HEAD] for n in range(4)]
        )
    for t in range(PARTS):
        rows = slice(t % 4 * 8, t % 4 * 8 + 8)
        block = [found[b][t // 4][rows] for b in range(ROWS)] + [stats[t * 8 : (t + 1) * 8]]
        packed[t] = jnp.concatenate(block, axis=0).astype(BF16)


def fresh_body(
    place, near, near_1, near_2, near_3, low, own, cosines, sines, gain,
    weighted, stats_out, pieces,
):
    for k, piece in enumerate((near, near_1, near_2, near_3)):
        pieces[(place[0] % 4) ^ k] = piece[...]
    ranks = [low[t].astype(F32)[0:12] for t in range(PARTS)]
    ranks = jnp.concatenate(ranks, axis=0)[:, 0:32].astype(BF16)
    fresh_key = []
    fresh_value = []
    for q in range(4):
        raw = unfold(pieces[q, 0:16].astype(F32))
        lift = unfold(pieces[q, 16:48].astype(F32)).astype(BF16)
        key = raw + ADAPTER_SCALE * dot(ranks[64:128], lift, (0, 0))
        value = raw + ADAPTER_SCALE * dot(ranks[128:192], lift, (0, 0))
        fresh_key.append(key[:, 0:32])
        fresh_value.append(value[:, 32:64])
    new_keys = jnp.concatenate(fresh_key, axis=1).astype(BF16).astype(F32)
    scale = gain[...].astype(F32).reshape(1, -1)
    new_keys = rms_rope(new_keys, scale, cosines[...], sines[...]).astype(BF16)
    new_values = jnp.concatenate(fresh_value, axis=1).astype(BF16)
    scores = dot(own[...], new_keys, (1, 1)) * SCALING
    row, col = iotas((64, 32))
    usable = (row // 8 == col // TOKENS) & (col % TOKENS <= row % TOKENS)
    highest, weights, total = softmax_parts(scores, usable)
    weighted[...] = dot(weights, new_values)
    _, lane = iotas((8, 128))
    stats = jnp.zeros((8, 128), F32)
    for b in range(ROWS):
        stats = jnp.where(lane == b, highest[b * 8 : (b + 1) * 8], stats)
        stats = jnp.where(lane == 8 + b, total[b * 8 : (b + 1) * 8], stats)
    stats_out[...] = stats


def load_body(source, held, sem):
    copy = pltpu.make_async_copy(source, held, sem)
    copy.start()
    copy.wait()


def output_body(
    gathered, own_weighted, own_stats, output_w, out_down, packed
):
    blocks = [gathered[t].astype(F32) for t in range(PARTS)]
    stats = [block[64:72] for block in blocks] + [own_stats[...]]
    values = [block[0:64] for block in blocks] + [own_weighted[...]]
    highest = functools.reduce(jnp.maximum, stats)
    factors = [jnp.exp(jnp.minimum(s - highest, 0.0)) for s in stats]
    total = jnp.zeros((8, 128), F32)
    for s, f in zip(stats, factors):
        total = total + f * (pltpu.roll(s, 120, 1) + pltpu.roll(s, 112, 1))
    _, lane = iotas((8, 128))
    inverse = 1.0 / jnp.where(lane < 8, total, 1.0)
    pieces = []
    for b in range(ROWS):
        piece = jnp.zeros((8, 128), F32)
        for v, f in zip(values, factors):
            piece = piece + f[:, b : b + 1] * v[b * 8 : (b + 1) * 8]
        pieces.append(piece * inverse[:, b : b + 1])
    heads = jnp.concatenate(pieces, axis=0).astype(BF16)
    heads = dot(regroup(2, 8), heads).astype(BF16)
    heads = jnp.concatenate([heads[0:32], heads[32:64]], axis=1)
    low = dot(heads, out_down[...], (1, 1))
    partial = dot(heads, output_w[...])
    for t in range(PARTS):
        block = jnp.concatenate([partial[:, t * 320 : (t + 1) * 320], low], axis=1)
        packed[t] = block.astype(BF16)


def finish_body(gathered, out_up, result):
    total = gathered[0].astype(F32)
    for t in range(1, PARTS):
        total = total + gathered[t].astype(F32)
    update = dot(total[:, 320:384].astype(BF16), out_up[...])
    out = total[:, 0:320] + ADAPTER_SCALE * update[:, 0:320]
    result[...] = out.reshape(ROWS, TOKENS, 320).astype(BF16)


def swap(block, axis):
    return lax.all_to_all(block, axis, 0, 0)


def local(
    layer_inputs,
    input_norm_gain,
    query_norm_gain,
    key_norm_gain,
    query_matrix,
    key_matrix,
    value_matrix,
    output_matrix,
    adapter_down,
    query_up_factor,
    key_up_factor,
    value_up_factor,
    output_down_factor,
    output_up_factor,
    stored_keys,
    stored_values,
    filled_lengths,
):
    dma = pltpu.SemaphoreType.DMA
    width = layer_inputs.shape[-1]
    place = lax.axis_index("tp").astype(jnp.int32).reshape(1)
    shards = (
        adapter_down.T,
        output_down_factor.T,
        query_up_factor,
        key_up_factor,
        value_up_factor,
        output_up_factor,
    )
    packed = call(
        pack_body,
        SHAPE((GROUPS, 24, 384), BF16),
        shards,
        "aaaaaa",
        8,
        [pltpu.VMEM(s.shape, BF16) for s in shards] + [dma((6,))],
    )
    packed, place = lax.optimization_barrier((packed, place))
    packed = swap(packed, "group")

    inverse = THETA ** (-(np.arange(64, dtype=np.float64) * 2.0 / HEAD))
    inverse = jnp.asarray(np.concatenate([inverse, inverse]).reshape(1, HEAD), F32)
    normed, cosines, sines, base, fresh = call(
        prepare_body,
        (
            SHAPE((32, width), BF16),
            SHAPE((32, HEAD), F32),
            SHAPE((32, HEAD), F32),
            SHAPE((32, 256), F32),
            SHAPE((32, HEAD), F32),
        ),
        (
            filled_lengths,
            layer_inputs,
            input_norm_gain,
            inverse,
            query_matrix,
            key_matrix.T,
            value_matrix.T,
        ),
        "saaaaaa",
        10.75,
        [
            pltpu.VMEM(layer_inputs.shape, BF16),
            pltpu.VMEM((width,), BF16),
            pltpu.VMEM((1, HEAD), F32),
            pltpu.VMEM(query_matrix.shape, BF16),
            pltpu.VMEM((32, width), BF16),
            pltpu.VMEM((32, width), BF16),
            dma((5 + CHUNKS,)),
        ],
        moved=WINDOW,
    )
    low, near = call(
        low_body,
        (SHAPE((PARTS, 16, 128), BF16), SHAPE((48, 128), BF16)),
        (packed, normed, fresh),
        "vvv",
        20,
    )
    low = swap(low, "tp")
    near = [near] + [
        lax.ppermute(near, "tp", [(i, i ^ k) for i in range(PARTS)]) for k in range(1, 4)
    ]
    low, near = lax.optimization_barrier((low, near))
    queries, own = call(
        query_body,
        (SHAPE((PARTS, 64, 128), BF16), SHAPE((64, 128), BF16)),
        (low, packed, base, cosines, sines, query_norm_gain),
        "vvvvvv",
        20,
    )
    gathered = swap(queries, "tp")
    parts = call(
        attend_body,
        SHAPE((PARTS, 72, 128), BF16),
        (place, filled_lengths, gathered, stored_keys, stored_values),
        "ssvvv",
        20,
    )
    parts, own, output_late, late = lax.optimization_barrier(
        (parts, own, output_matrix, packed)
    )
    parts = swap(parts, "tp")
    output_late = call(
        load_body, SHAPE(output_matrix.shape, BF16), (output_late,), "a", 14, [dma], moved=WINDOW
    )
    out_down, out_up = call(
        unpack_body,
        (SHAPE((64, 256), BF16), SHAPE((64, 384), BF16)),
        (late,),
        "v",
        20,
        moved=WINDOW,
    )
    own_weighted, own_stats = call(
        fresh_body,
        (SHAPE((64, 128), F32), SHAPE((8, 128), F32)),
        (place, *near, low, own, cosines, sines, key_norm_gain),
        "svvvvvvvvv",
        20,
        [pltpu.VMEM((4, 48, 128), BF16)],
        moved=WINDOW,
    )
    partial = call(
        output_body,
        SHAPE((PARTS, 32, 384), BF16),
        (parts, own_weighted, own_stats, output_late, out_down),
        "vvvvv",
        20,
    )
    partial = swap(partial, "tp")
    return call(finish_body, SHAPE((ROWS, TOKENS, 320), BF16), (partial, out_up), "vv", 20)


def solution(mesh):
    in_specs = (
        P("group", None, None),
        P(),
        P(),
        P(),
        P(None, "tp"),
        P(None, "tp"),
        P(None, "tp"),
        P("tp", None),
        P("group", "tp"),
        P("group", "tp"),
        P("group", "tp"),
        P("group", "tp"),
        P("tp", "group"),
        P("group", "tp"),
        P("group", "tp", None),
        P("group", "tp", None),
        P("group"),
    )
    out_specs = P("group", None, "tp")
    return jax.shard_map(local, mesh=mesh, in_specs=in_specs, out_specs=out_specs, check_vma=False)
```

```python
import functools
import math

import jax
import jax.numpy as jnp
import numpy as np
from jax import lax
from jax.experimental import pallas as pl
from jax.experimental.pallas import tpu as pltpu
from jax.sharding import PartitionSpec as P

EPS = 1e-06
ADAPTER_SCALE = 2.0
THETA = 1000000.0
GROUPS = 16
PARTS = 16
HEAD = 128
TOKENS = 4
ROWS = 8
F32 = jnp.float32
BF16 = jnp.bfloat16
SHAPE = jax.ShapeDtypeStruct
WINDOW = 16 * 2**20


def call(body, out_shapes, args, spaces, room, scratch=(), left=(), moved=0):
    places = {"s": pltpu.SMEM, "a": pltpu.HBM, "v": pltpu.VMEM}
    specs = [pl.BlockSpec(memory_space=places[c]) for c in spaces]
    many = isinstance(out_shapes, tuple)
    outs = [
        pl.BlockSpec(memory_space=pltpu.HBM if i in left else pltpu.VMEM)
        for i in range(len(out_shapes) if many else 1)
    ]
    return pl.pallas_call(
        body,
        out_shape=out_shapes,
        in_specs=specs,
        out_specs=tuple(outs) if many else outs[0],
        scratch_shapes=list(scratch),
        compiler_params=pltpu.CompilerParams(vmem_limit_bytes=int((64 - room) * 2**20)),
        cost_estimate=pl.CostEstimate(flops=0, bytes_accessed=moved, transcendentals=0),
    )(*args)


def dot(a, b, contract=(1, 0)):
    return lax.dot_general(
        a, b, (((contract[0],), (contract[1],)), ((), ())), preferred_element_type=F32
    )


def widen(block, lanes):
    return jnp.concatenate(
        [block, jnp.zeros((block.shape[0], lanes - block.shape[1]), block.dtype)], axis=1
    )


def iotas(shape):
    return [lax.broadcasted_iota(jnp.int32, shape, d) for d in range(2)]


def fetch(sources, held, sems):
    copies = [pltpu.make_async_copy(s, h, sems.at[i]) for i, (s, h) in enumerate(zip(sources, held))]
    for copy in copies:
        copy.start()
    return copies


def pack_body(*refs):
    packed, held = refs[6], refs[7:13]
    for copy in fetch(refs[:6], held, refs[13]):
        copy.wait()
    down, out_down, query_up, key_up, value_up, out_up = [h[...].astype(F32) for h in held]
    up = jnp.concatenate([query_up, key_up, value_up], axis=1)
    block = jnp.concatenate(
        [widen(down, 384), widen(out_down, 384), widen(up, 384), widen(out_up, 384)], axis=0
    ).astype(BF16)
    for i in range(GROUPS):
        packed[i] = block


CHUNKS = 4


def prepare_body(
    lengths, x_any, gain_any, inverse_any, query_any, key_any, value_any,
    normed, cosines, sines, base, fresh, x_ref, gain, inverse, query_w, key_w, value_w, sems,
):
    step = query_any.shape[0] // CHUNKS
    rows = [pl.ds(c * step, step) for c in range(CHUNKS)]
    copies = fetch(
        [x_any, gain_any, inverse_any, key_any, value_any] + [query_any.at[r] for r in rows],
        [x_ref, gain, inverse, key_w, value_w] + [query_w.at[r] for r in rows],
        sems,
    )
    for copy in copies[:3]:
        copy.wait()
    x = x_ref[...].astype(F32).reshape(ROWS * TOKENS, -1)
    scale = lax.rsqrt(jnp.mean(x * x, axis=-1, keepdims=True) + EPS)
    value = (x * scale * gain[...].astype(F32).reshape(1, -1)).astype(BF16)
    normed[...] = value
    row, lane = iotas((ROWS * TOKENS, HEAD))
    position = row % TOKENS
    for b in range(ROWS):
        position = position + jnp.where(row // TOKENS == b, lengths[b], 0)
    angles = position.astype(F32) * inverse[...]
    cosines[...] = jnp.cos(angles)
    sines[...] = jnp.where(lane < 64, -1.0, 1.0) * jnp.sin(angles)
    copies[3].wait()
    copies[4].wait()
    both = jnp.concatenate([key_w[...], value_w[...]], axis=0)
    fresh[...] = widen(dot(value, both, (1, 1)), 128)
    raw = jnp.zeros((32, 256), F32)
    for c in range(CHUNKS):
        copies[5 + c].wait()
        part = slice(c * step, (c + 1) * step)
        raw = raw + dot(value[:, part], query_w[part, :])
    base[...] = raw


def fold(block):
    rows = block.shape[0] // 2
    _, lane = iotas((rows, 128))
    return jnp.where(lane < 64, block[0:rows], pltpu.roll(block[rows:], 64, 1))


def unfold(block):
    return jnp.concatenate([block, pltpu.roll(block, 64, 1)], axis=0)


def low_body(packed, normed, fresh, low, near):
    pieces = [packed[g].astype(F32) for g in range(GROUPS)]
    down = jnp.concatenate([p[0:16, 0:320] for p in pieces], axis=1).astype(BF16)
    block = widen(dot(down, normed[...], (1, 1)), 128).astype(BF16)
    for t in range(PARTS):
        low[t] = block
    lift = jnp.concatenate([p[16:20, 256:384] for p in pieces], axis=0)
    near[0:16] = fold(fresh[...]).astype(BF16)
    near[16:48] = fold(lift).astype(BF16)


def unpack_body(packed, out_down, out_up):
    pieces = [packed[g].astype(F32) for g in range(GROUPS)]
    out_down[...] = jnp.concatenate([p[12:16, 0:256] for p in pieces], axis=0).astype(BF16)
    out_up[...] = jnp.concatenate([p[20:24] for p in pieces], axis=0).astype(BF16)


def rms_rope(heads, gain, cosines, sines):
    scale = lax.rsqrt(jnp.mean(heads * heads, axis=-1, keepdims=True) + EPS)
    heads = heads * scale * gain
    return heads * cosines + pltpu.roll(heads, 64, 1) * sines


def regroup(count_from, count_to):
    row, col = iotas((64, 64))
    source = ((row // TOKENS) % count_to) * (count_from * TOKENS)
    source = source + (row // (TOKENS * count_to)) * TOKENS + row % TOKENS
    return jnp.where(col == source, 1.0, 0.0).astype(BF16)


def query_body(low, packed, base, cosines, sines, gain, sent, own):
    ranks = jnp.concatenate([low[t].astype(F32)[0:12] for t in range(6)], axis=0)
    ranks = ranks[0:64, 0:32].astype(BF16)
    lift = [packed[g].astype(F32)[16:20, 0:256] for g in range(GROUPS)]
    update = dot(ranks, jnp.concatenate(lift, axis=0).astype(BF16), (0, 0))
    raw = base[...] + ADAPTER_SCALE * update
    scale = gain[...].astype(F32).reshape(1, -1)
    heads = [
        rms_rope(raw[:, j * HEAD : (j + 1) * HEAD], scale, cosines[...], sines[...])
        for j in range(2)
    ]
    queries = jnp.concatenate(heads, axis=0).astype(BF16)
    queries = dot(regroup(8, 2), queries).astype(BF16)
    for i in range(PARTS):
        sent[i] = queries
    own[...] = queries


def softmax_parts(scores, usable):
    masked = jnp.where(usable, scores, -1e30)
    highest = jnp.maximum(jnp.max(masked, axis=-1, keepdims=True), -1e29)
    highest = highest.astype(BF16).astype(F32)
    weights = jnp.exp(masked - highest).astype(BF16)
    total = jnp.sum(weights.astype(F32), axis=-1, keepdims=True)
    return highest, weights, total


SCALING = 1.0 / math.sqrt(HEAD)
SPAN = 128


def attend_body(place, lengths, gathered, keys, values, packed):
    offset = place[0] * SPAN
    everything = [gathered[t].astype(F32) for t in range(PARTS)]
    _, lane = iotas((128, 128))
    stats = jnp.zeros((128, 128), F32)
    empty = jnp.zeros((32, 128), BF16)
    found = []
    for b in range(ROWS):
        query = jnp.concatenate(
            [q[b * 8 : (b + 1) * 8] for q in everything], axis=0
        ).astype(BF16)
        query = jnp.concatenate(
            [
                jnp.concatenate(
                    [query[n * 32 : (n + 1) * 32] if m == n else empty for m in range(4)], axis=1
                )
                for n in range(4)
            ],
            axis=0,
        )
        scores = dot(query, keys[b], (1, 1))
        highest, weights, total = softmax_parts(scores * SCALING, lane + offset < lengths[b])
        total_high = total.astype(BF16).astype(F32)
        stats = jnp.where(lane == b, highest, stats)
        stats = jnp.where(lane == 8 + b, total_high, stats)
        stats = jnp.where(lane == 16 + b, total - total_high, stats)
        weighted = dot(weights, values[b])
        found.append(
            [weighted[n * 32 : (n + 1) * 32, n * HEAD : (n + 1) * HEAD] for n in range(4)]
        )
    for t in range(PARTS):
        rows = slice(t % 4 * 8, t % 4 * 8 + 8)
        block = [found[b][t // 4][rows] for b in range(ROWS)] + [stats[t * 8 : (t + 1) * 8]]
        packed[t] = jnp.concatenate(block, axis=0).astype(BF16)


def fresh_body(
    place, near, near_1, near_2, near_3, low, own, cosines, sines, gain,
    weighted, stats_out, pieces,
):
    for k, piece in enumerate((near, near_1, near_2, near_3)):
        pieces[(place[0] % 4) ^ k] = piece[...]
    ranks = [low[t].astype(F32)[0:12] for t in range(PARTS)]
    ranks = jnp.concatenate(ranks, axis=0)[:, 0:32].astype(BF16)
    fresh_key = []
    fresh_value = []
    for q in range(4):
        raw = unfold(pieces[q, 0:16].astype(F32))
        lift = unfold(pieces[q, 16:48].astype(F32)).astype(BF16)
        key = raw + ADAPTER_SCALE * dot(ranks[64:128], lift, (0, 0))
        value = raw + ADAPTER_SCALE * dot(ranks[128:192], lift, (0, 0))
        fresh_key.append(key[:, 0:32])
        fresh_value.append(value[:, 32:64])
    new_keys = jnp.concatenate(fresh_key, axis=1).astype(BF16).astype(F32)
    scale = gain[...].astype(F32).reshape(1, -1)
    new_keys = rms_rope(new_keys, scale, cosines[...], sines[...]).astype(BF16)
    new_values = jnp.concatenate(fresh_value, axis=1).astype(BF16)
    scores = dot(own[...], new_keys, (1, 1)) * SCALING
    row, col = iotas((64, 32))
    usable = (row // 8 == col // TOKENS) & (col % TOKENS <= row % TOKENS)
    highest, weights, total = softmax_parts(scores, usable)
    weighted[...] = dot(weights, new_values)
    _, lane = iotas((8, 128))
    stats = jnp.zeros((8, 128), F32)
    for b in range(ROWS):
        stats = jnp.where(lane == b, highest[b * 8 : (b + 1) * 8], stats)
        stats = jnp.where(lane == 8 + b, total[b * 8 : (b + 1) * 8], stats)
    stats_out[...] = stats


def load_body(source, held, sem):
    copy = pltpu.make_async_copy(source, held, sem)
    copy.start()
    copy.wait()


def output_body(
    gathered, own_weighted, own_stats, output_w, out_down, packed
):
    blocks = [gathered[t].astype(F32) for t in range(PARTS)]
    stats = [block[64:72] for block in blocks] + [own_stats[...]]
    values = [block[0:64] for block in blocks] + [own_weighted[...]]
    highest = functools.reduce(jnp.maximum, stats)
    factors = [jnp.exp(jnp.minimum(s - highest, 0.0)) for s in stats]
    total = jnp.zeros((8, 128), F32)
    for s, f in zip(stats, factors):
        total = total + f * (pltpu.roll(s, 120, 1) + pltpu.roll(s, 112, 1))
    _, lane = iotas((8, 128))
    inverse = 1.0 / jnp.where(lane < 8, total, 1.0)
    pieces = []
    for b in range(ROWS):
        piece = jnp.zeros((8, 128), F32)
        for v, f in zip(values, factors):
            piece = piece + f[:, b : b + 1] * v[b * 8 : (b + 1) * 8]
        pieces.append(piece * inverse[:, b : b + 1])
    heads = jnp.concatenate(pieces, axis=0).astype(BF16)
    heads = dot(regroup(2, 8), heads).astype(BF16)
    heads = jnp.concatenate([heads[0:32], heads[32:64]], axis=1)
    low = dot(heads, out_down[...], (1, 1))
    partial = dot(heads, output_w[...])
    for t in range(PARTS):
        block = jnp.concatenate([partial[:, t * 320 : (t + 1) * 320], low], axis=1)
        packed[t] = block.astype(BF16)


def finish_body(gathered, out_up, result):
    total = gathered[0].astype(F32)
    for t in range(1, PARTS):
        total = total + gathered[t].astype(F32)
    update = dot(total[:, 320:384].astype(BF16), out_up[...])
    out = total[:, 0:320] + ADAPTER_SCALE * update[:, 0:320]
    result[...] = out.reshape(ROWS, TOKENS, 320).astype(BF16)


def swap(block, axis):
    return lax.all_to_all(block, axis, 0, 0)


def local(
    layer_inputs,
    input_norm_gain,
    query_norm_gain,
    key_norm_gain,
    query_matrix,
    key_matrix,
    value_matrix,
    output_matrix,
    adapter_down,
    query_up_factor,
    key_up_factor,
    value_up_factor,
    output_down_factor,
    output_up_factor,
    stored_keys,
    stored_values,
    filled_lengths,
):
    dma = pltpu.SemaphoreType.DMA
    width = layer_inputs.shape[-1]
    place = lax.axis_index("tp").astype(jnp.int32).reshape(1)
    shards = (
        adapter_down.T,
        output_down_factor.T,
        query_up_factor,
        key_up_factor,
        value_up_factor,
        output_up_factor,
    )
    packed = call(
        pack_body,
        SHAPE((GROUPS, 24, 384), BF16),
        shards,
        "aaaaaa",
        8,
        [pltpu.VMEM(s.shape, BF16) for s in shards] + [dma((6,))],
    )
    packed, place = lax.optimization_barrier((packed, place))
    packed = swap(packed, "group")

    inverse = THETA ** (-(np.arange(64, dtype=np.float64) * 2.0 / HEAD))
    inverse = jnp.asarray(np.concatenate([inverse, inverse]).reshape(1, HEAD), F32)
    normed, cosines, sines, base, fresh = call(
        prepare_body,
        (
            SHAPE((32, width), BF16),
            SHAPE((32, HEAD), F32),
            SHAPE((32, HEAD), F32),
            SHAPE((32, 256), F32),
            SHAPE((32, HEAD), F32),
        ),
        (
            filled_lengths,
            layer_inputs,
            input_norm_gain,
            inverse,
            query_matrix,
            key_matrix.T,
            value_matrix.T,
        ),
        "saaaaaa",
        10.75,
        [
            pltpu.VMEM(layer_inputs.shape, BF16),
            pltpu.VMEM((width,), BF16),
            pltpu.VMEM((1, HEAD), F32),
            pltpu.VMEM(query_matrix.shape, BF16),
            pltpu.VMEM((32, width), BF16),
            pltpu.VMEM((32, width), BF16),
            dma((5 + CHUNKS,)),
        ],
        moved=WINDOW,
    )
    low, near = call(
        low_body,
        (SHAPE((PARTS, 16, 128), BF16), SHAPE((48, 128), BF16)),
        (packed, normed, fresh),
        "vvv",
        20,
    )
    low = swap(low, "tp")
    near = [near] + [
        lax.ppermute(near, "tp", [(i, i ^ k) for i in range(PARTS)]) for k in range(1, 4)
    ]
    queries, own = call(
        query_body,
        (SHAPE((PARTS, 64, 128), BF16), SHAPE((64, 128), BF16)),
        (low, packed, base, cosines, sines, query_norm_gain),
        "vvvvvv",
        20,
    )
    gathered = swap(queries, "tp")
    parts = call(
        attend_body,
        SHAPE((PARTS, 72, 128), BF16),
        (place, filled_lengths, gathered, stored_keys, stored_values),
        "ssvvv",
        20,
    )
    parts, own, output_late, late = lax.optimization_barrier(
        (parts, own, output_matrix, packed)
    )
    parts = swap(parts, "tp")
    output_late = call(
        load_body, SHAPE(output_matrix.shape, BF16), (output_late,), "a", 14, [dma], moved=WINDOW
    )
    out_down, out_up = call(
        unpack_body,
        (SHAPE((64, 256), BF16), SHAPE((64, 384), BF16)),
        (late,),
        "v",
        20,
        moved=WINDOW,
    )
    own_weighted, own_stats = call(
        fresh_body,
        (SHAPE((64, 128), F32), SHAPE((8, 128), F32)),
        (place, *near, low, own, cosines, sines, key_norm_gain),
        "svvvvvvvvv",
        20,
        [pltpu.VMEM((4, 48, 128), BF16)],
        moved=WINDOW,
    )
    partial = call(
        output_body,
        SHAPE((PARTS, 32, 384), BF16),
        (parts, own_weighted, own_stats, output_late, out_down),
        "vvvvv",
        20,
    )
    partial = swap(partial, "tp")
    return call(finish_body, SHAPE((ROWS, TOKENS, 320), BF16), (partial, out_up), "vv", 20)


def solution(mesh):
    in_specs = (
        P("group", None, None),
        P(),
        P(),
        P(),
        P(None, "tp"),
        P(None, "tp"),
        P(None, "tp"),
        P("tp", None),
        P("group", "tp"),
        P("group", "tp"),
        P("group", "tp"),
        P("group", "tp"),
        P("tp", "group"),
        P("group", "tp"),
        P("group", "tp", None),
        P("group", "tp", None),
        P("group"),
    )
    out_specs = P("group", None, "tp")
    return jax.shard_map(local, mesh=mesh, in_specs=in_specs, out_specs=out_specs, check_vma=False)
```
